32 devices in a mesh: grp: 2 (over x), space: 16 (over z, y, core).
Axes of the slice: x: 2, y: 2, z: 4, core: 2. Of those that a mesh axis runs over, the one named last changes fastest.
Arguments:
- right_side: float32 [165, 12288], P(None, ('grp', 'space')), parts along dimension 1, may hold values from -48 to 48
- capacity: float32 [12288], P(('grp', 'space')), parts along dimension 0, may hold values from 0.5 to 2
- base_cond: float32 [192, 24, 4096], P(('grp', 'space')), parts along dimension 0, may hold values from 0.0005 to 0.005
- var_field: float32 [8, 12288], P(None, ('grp', 'space')), parts along dimension 1, may hold values from -1 to 1
- block_cols: int32 [192, 23], P(('grp', 'space')), parts along dimension 0, may hold values from 0 to 11, as said below
- send_list: int32 [32, 2, 3], P(('grp', 'space')), parts along dimension 0, may hold values from 0 to 5, as said below
Outputs:
- solution_field: float32 [165, 12288], P(None, ('grp', 'space')), parts along dimension 1
- residual: float32 [165, 12288], P(None, ('grp', 'space')), parts along dimension 1
The draws below stay inside these ranges and needn't reach their ends.
There are 2 independent parts, one for each index of `grp`. The reference program is written for one: setup_inputs(seed, part) draws one part's arguments, and reference() takes and returns one part's arrays. A program takes and returns all parts, laid end to end along the dimension named above; each array names one. Nothing has to cross between parts.
Inputs may be any that keep to these rules, and one draw needn't show every extreme that they name: `block_cols`: A value below 6 names a block of the same device; 6 + h names the h-th block that the previous device of space sends up, 9 + h the h-th block that the next device sends down. The first device never names the previous one, the last never names the next one; every other value occurs on every device. `send_list`: on every device the 6 blocks differ; block 5 is always sent up and block 0 always sent down.
All inputs are finite; a program needn't handle non-finite values.
Results may differ from the reference program's by a relative error of at most 0.0003.
Values sent between devices are 32-bit elements; how exact they have to be, the bound alone decides.
A program may use at most 128 MiB of HBM per device.

```python
import math
import jax
import jax.numpy as jnp
import numpy as np
from jax import lax

VARS = 8
ORDER = 3
TERMS = 165
MODES = 9
BLK = 64
SLOTS = 24
HALO = 3
NB_DEV = 6
ITERS = 2
NBLOCKS = 96
NODES = 6144
N_SPACE = 16


def draw_right_side(key, part):
    key_core = jax.random.fold_in(key, 11)
    key_node = jax.random.fold_in(key, 12)
    key_term = jax.random.fold_in(key, 13)
    along = jnp.arange(NODES, dtype=jnp.float32) / (NODES - 1)
    node_scale = 10.0 ** (jax.random.uniform(key_node, (NODES,), jnp.float32) - 0.5)
    term_scale = 10.0 ** (jax.random.uniform(key_term, (TERMS, 1), jnp.float32) - 0.5)
    core = jnp.clip(jax.random.normal(key_core, (TERMS, NODES), jnp.float32), -3.0, 3.0)
    rising = 3.0 ** (along - 0.5)
    return (core * node_scale * rising * term_scale * 0.5).astype(jnp.float32)


def draw_block_cols(key, part):
    extent_ids = NB_DEV + 2 * HALO
    positions = NB_DEV * (SLOTS - 1)
    repeats = -(-positions // extent_ids)

    def one_device(device_key, device):
        pieces = [jax.random.permutation(jax.random.fold_in(device_key, t), extent_ids) for t in range(repeats)]
        sequence = jnp.concatenate(pieces)[:positions].astype(jnp.int32)
        lower_bad = (sequence >= NB_DEV) & (sequence < NB_DEV + HALO) & (device == 0)
        upper_bad = (sequence >= NB_DEV + HALO) & (device == N_SPACE - 1)
        sequence = jnp.where(lower_bad | upper_bad, sequence % NB_DEV, sequence)
        sequence = jax.random.permutation(jax.random.fold_in(device_key, 1000), sequence)
        return sequence.reshape(NB_DEV, SLOTS - 1)
    devices = jnp.arange(N_SPACE, dtype=jnp.int32)
    device_keys = jax.vmap(lambda d: jax.random.fold_in(key, d))(devices)
    return jax.vmap(one_device)(device_keys, devices).reshape(N_SPACE * NB_DEV, SLOTS - 1).astype(jnp.int32)


def draw_send_list(key, part):

    def one_device(device_key):
        ranks = jax.random.permutation(device_key, NB_DEV).astype(jnp.int32)
        places = jnp.arange(NB_DEV, dtype=jnp.int32)
        ranks = jnp.where(places == 0, -2, jnp.where(places == NB_DEV - 1, -1, ranks))
        order = jnp.argsort(ranks, stable=True).astype(jnp.int32)
        upward = order[1:HALO + 1]
        downward = jnp.concatenate([order[0:1], order[HALO + 1:2 * HALO]])
        return jnp.stack([upward, downward], axis=0)
    device_keys = jax.vmap(lambda d: jax.random.fold_in(jax.random.fold_in(key, 77), d))(jnp.arange(N_SPACE))
    return jax.vmap(one_device)(device_keys).astype(jnp.int32)


def block_scale(stream_key, dims, cuts, least, high):
    factor_of = 1.0
    for position, blocks in cuts:
        draws = jax.random.uniform(jax.random.fold_in(jax.random.fold_in(stream_key, 6), position), (blocks,), jnp.float32, least / len(cuts), high / len(cuts))
        factor_of = factor_of * jnp.repeat(jnp.exp(draws), dims[position] // blocks).reshape((-1,) + (1,) * (len(dims) - 1 - position))
    return factor_of


def setup_inputs(seed: int = 0, part: int = 0) -> dict:
    keys = jax.random.split(jax.random.key(seed), 7)
    part_keys = jax.random.split(jax.random.fold_in(keys[6], part), 7)
    return {
        "right_side": draw_right_side(jax.random.fold_in(jax.random.fold_in(keys[6], part), 71), part),
        "capacity": jnp.clip(jnp.exp(math.log(2.0) - 1.3862944 * jax.random.uniform(part_keys[1], (NODES,), jnp.float32) ** block_scale(part_keys[1], (NODES,), ((0, 16),), -0.2, 0.2)), 0.5, 2.0),
        "base_cond": jnp.clip(jnp.exp(math.log(0.005) - 2.30258502 * jax.random.uniform(part_keys[2], (NBLOCKS, SLOTS, BLK * BLK), jnp.float32) ** block_scale(part_keys[2], (NBLOCKS, SLOTS, BLK * BLK), ((0, 16),), -0.2, 0.2)), 0.0005, 0.005),
        "var_field": jnp.clip(jax.random.uniform(part_keys[3], (VARS, NODES), jnp.float32, -1.0, 1.0) * block_scale(part_keys[3], (VARS, NODES), ((1, 16),), -0.4, 0.0), -1.0, 1.0),
        "block_cols": draw_block_cols(jax.random.fold_in(jax.random.fold_in(keys[6], part), 71), part),
        "send_list": draw_send_list(jax.random.fold_in(jax.random.fold_in(keys[6], part), 71), part),
    }


spread_coefficient = 0.14

def chaos_tables():
    entries = []

    def grow(prefix, budget_left):
        if len(prefix) == VARS:
            entries.append(tuple(prefix))
            return
        for degree in range(budget_left + 1):
            grow(prefix + [degree], budget_left - degree)
    grow([], ORDER)
    entries.sort(key=lambda multi_index: (sum(multi_index), tuple((-v for v in multi_index))))
    lookup = {multi_index: place for place, multi_index in enumerate(entries)}
    count_terms = len(entries)
    down_index = np.full((VARS, count_terms), count_terms, np.int32)
    down_scale = np.zeros((VARS, count_terms), np.float32)
    up_index = np.full((VARS, count_terms), count_terms, np.int32)
    up_scale = np.zeros((VARS, count_terms), np.float32)
    for place, multi_index in enumerate(entries):
        for k in range(VARS):
            if multi_index[k] > 0:
                lowered = multi_index[:k] + (multi_index[k] - 1,) + multi_index[k + 1:]
                down_index[k, place] = lookup[lowered]
                down_scale[k, place] = math.sqrt(multi_index[k])
            raised = multi_index[:k] + (multi_index[k] + 1,) + multi_index[k + 1:]
            if raised in lookup:
                up_index[k, place] = lookup[raised]
                up_scale[k, place] = math.sqrt(multi_index[k] + 1)
    return (down_index, down_scale, up_index, up_scale)

def couple(field, mode_weights):
    down_index, down_scale, up_index, up_scale = chaos_tables()
    padded = jnp.concatenate([field, jnp.zeros((1,) + field.shape[1:], field.dtype)], axis=0)
    total = mode_weights[0] * field
    for k in range(VARS):
        lowered = jnp.take(padded, down_index[k], axis=0) * down_scale[k][:, None, None]
        raised = jnp.take(padded, up_index[k], axis=0) * up_scale[k][:, None, None]
        total = total + mode_weights[k + 1] * (lowered + raised)
    return total

def reference(right_side, capacity, base_cond, var_field, block_cols, send_list):
    blocks = NB_DEV * N_SPACE
    base_cond = base_cond.reshape(blocks, SLOTS, BLK, BLK)
    owner = jnp.arange(blocks, dtype=jnp.int32) // NB_DEV
    own_index = jnp.arange(blocks, dtype=jnp.int32) % NB_DEV
    local_ids = jnp.concatenate([own_index[:, None], block_cols], axis=1)
    lower_slot = jnp.clip(local_ids - NB_DEV, 0, HALO - 1)
    upper_slot = jnp.clip(local_ids - NB_DEV - HALO, 0, HALO - 1)
    lower_peer = jnp.clip(owner - 1, 0, N_SPACE - 1)[:, None]
    upper_peer = jnp.clip(owner + 1, 0, N_SPACE - 1)[:, None]
    from_lower = lower_peer * NB_DEV + send_list[lower_peer, 0, lower_slot]
    from_upper = upper_peer * NB_DEV + send_list[upper_peer, 1, upper_slot]
    columns = jnp.where(local_ids < NB_DEV, owner[:, None] * NB_DEV + local_ids, jnp.where(local_ids < NB_DEV + HALO, from_lower, from_upper)).astype(jnp.int32)
    mode_weights = jnp.concatenate([jnp.ones((1, NODES), jnp.float32), spread_coefficient * var_field], axis=0)
    mode_weights = mode_weights.reshape(MODES, blocks, BLK)
    row_total = lax.optimization_barrier(jnp.sum(base_cond, axis=(1, 3)))
    column_total = jnp.einsum('rsab,mra->mrsb', base_cond, mode_weights, precision=lax.Precision.HIGHEST)
    transfer = jnp.zeros((MODES, blocks, BLK), jnp.float32).at[:, columns.reshape(-1)].add(column_total.reshape(MODES, blocks * SLOTS, BLK))
    cap_blocks = capacity.reshape(blocks, BLK)

    def operate(field):

        def group_step(accum, g):
            start = g * NB_DEV
            piece = lax.dynamic_slice_in_dim(field, start, NB_DEV, 1)
            group_cols = lax.dynamic_slice_in_dim(columns, start, NB_DEV, 0)
            group_base = lax.dynamic_slice_in_dim(base_cond, start, NB_DEV, 0)
            group_weights = lax.dynamic_slice_in_dim(mode_weights, start, NB_DEV, 1)
            group_rows = lax.dynamic_slice_in_dim(row_total, start, NB_DEV, 0)
            neighbours = jnp.take(field, group_cols, axis=1)
            outflow = group_rows * piece - jnp.einsum('rsab,prsb->pra', group_base, neighbours, precision=lax.Precision.HIGHEST)
            forward = couple(outflow, group_weights)
            coupled = couple(piece, group_weights)
            inflow = jnp.einsum('rsab,pra->prsb', group_base, coupled, precision=lax.Precision.HIGHEST)
            accum = accum.at[:, group_cols.reshape(-1)].add(-inflow.reshape(TERMS, NB_DEV * SLOTS, BLK))
            current = lax.dynamic_slice_in_dim(accum, start, NB_DEV, 1)
            accum = lax.dynamic_update_slice_in_dim(accum, current + forward, start, 1)
            return (accum, None)
        initial = cap_blocks * field + couple(field, transfer)
        result, unused = lax.scan(group_step, initial, jnp.arange(N_SPACE, dtype=jnp.int32))
        return result
    source_field = right_side.reshape(TERMS, blocks, BLK)
    solution_field = jnp.zeros_like(source_field)
    residual = source_field
    direction = source_field
    norm_now = jnp.sum(residual * residual)
    for step in range(ITERS):
        image = operate(direction)
        step_length = norm_now / jnp.sum(direction * image)
        solution_field = solution_field + step_length * direction
        residual = residual - step_length * image
        norm_next = jnp.sum(residual * residual)
        direction = residual + norm_next / norm_now * direction
        norm_now = norm_next
    return (solution_field.reshape(TERMS, NODES), residual.reshape(TERMS, NODES))
```

```python
import functools
import math

import jax
import jax.numpy as jnp
import numpy as np
from jax import lax
from jax.experimental import pallas as pl
from jax.experimental.pallas import tpu as pltpu
from jax.sharding import PartitionSpec as P

VARS = 8
ORDER = 3
ITERS = 2
SPREAD = 0.14
ROWS = 176
HALF = ROWS // 2
MSG = ROWS + HALF
MESH = pl.DeviceIdType.MESH
F32 = jnp.float32
BF16 = jnp.bfloat16


def chaos_tables():
    entries = []

    def grow(prefix, left):
        if len(prefix) == VARS:
            entries.append(tuple(prefix))
            return
        for degree in range(left + 1):
            grow(prefix + [degree], left - degree)

    grow([], ORDER)
    entries.sort(key=lambda m: (sum(m), tuple(-v for v in m)))
    lookup = {m: i for i, m in enumerate(entries)}
    coupling = np.zeros((VARS, ROWS, ROWS), np.float32)
    scale = np.ones((ROWS,), np.float64)
    for i, m in enumerate(entries):
        scale[i] = math.sqrt(math.prod(math.factorial(v) for v in m))
        for k in range(VARS):
            if m[k] > 0:
                coupling[k, i, lookup[m[:k] + (m[k] - 1,) + m[k + 1 :]]] = m[k]
            raised = m[:k] + (m[k] + 1,) + m[k + 1 :]
            if raised in lookup:
                coupling[k, i, lookup[raised]] = 1.0
    scales = np.stack([scale, 1.0 / scale**2, 1.0 / scale], 0)
    return coupling, np.broadcast_to(scales[:, :, None], (3, ROWS, 128)).astype(np.float32)


def split2(x):
    hi = x.astype(BF16)
    return hi, (x - hi.astype(F32)).astype(BF16)


def split3(x):
    hi = x.astype(BF16)
    rest = x - hi.astype(F32)
    mid = rest.astype(BF16)
    return hi, mid, (rest - mid.astype(F32)).astype(BF16)


def nn(a, b):
    return lax.dot_general(a, b, (((1,), (0,)), ((), ())), preferred_element_type=F32)


def nt(a, b):
    return lax.dot_general(a, b, (((1,), (1,)), ((), ())), preferred_element_type=F32)


def swap(x):
    return pltpu.roll(x, 64, 1)


def wide(x):
    return jnp.concatenate([x, x, x], axis=1)


def kernel(
    n,
    rhs_ref, var_ref, cap_ref, codes_ref, coup_ref, scale_ref, base_ref,
    x_ref, r_ref,
    inp, base, wc, wf, whi, wlo, ybuf, ext, lam, dmode, fieldb, gamb, cplb, qb, r1b, accb,
    fs, fr, hs, hr, ts, tr, allb,
    base_sem, send_sem, recv_sem, all_send, all_recv,
):
    me = lax.axis_index("space")
    prev, nxt = lax.rem(me + n - 1, n), lax.rem(me + 1, n)
    chunk = base.shape[1] // 4

    def base_copy(i):
        cols = pl.ds(i * chunk, chunk)
        return pltpu.make_async_copy(base_ref.at[:, cols], base.at[:, cols], base_sem.at[i])

    for i in range(4):
        base_copy(i).start()

    barrier = pltpu.get_barrier_semaphore()

    def greet(i, c):
        pl.semaphore_signal(
            barrier, inc=1, device_id={"space": lax.rem(me + i, n)}, device_id_type=MESH
        )
        return c

    lax.fori_loop(1, n, greet, 0)

    def remote(src, dst, which, peer):
        return pltpu.make_async_remote_copy(
            src_ref=src, dst_ref=dst, send_sem=send_sem.at[which], recv_sem=recv_sem.at[which],
            device_id={"space": peer}, device_id_type=MESH,
        )

    def pair(src, dst, e):
        up = remote(src.at[0], dst.at[0], 2 * e, nxt)
        down = remote(src.at[1], dst.at[1], 2 * e + 1, prev)
        return up, down

    def send(up, down):
        @pl.when(me < n - 1)
        def _():
            up.start()

        @pl.when(me > 0)
        def _():
            down.start()

    def arrive(up, down):
        @pl.when(me > 0)
        def _():
            up.wait_recv()

        @pl.when(me < n - 1)
        def _():
            down.wait_recv()

    def sent(up, down):
        @pl.when(me < n - 1)
        def _():
            up.wait_send()

        @pl.when(me > 0)
        def _():
            down.wait_send()

    def left_mask(rows):
        return lax.broadcasted_iota(jnp.int32, (rows, 128), 1) < 64

    def pack(dst, first, middle, last):
        rows = first.shape[0]
        half = rows // 2
        left = left_mask(half)
        top, low = middle[:half], middle[half:]
        dst[0, 0:rows] = first
        dst[0, rows : rows + half] = jnp.where(left, top, swap(low))
        dst[1, 0:rows] = last
        dst[1, rows : rows + half] = jnp.where(left, swap(top), low)

    def unpack(src, rows):
        half = rows // 2
        left = left_mask(half)
        up, down = src[0, rows : rows + half], src[1, rows : rows + half]
        middle = jnp.concatenate(
            [jnp.where(left, up, swap(down)), jnp.where(left, swap(up), down)], axis=0
        )
        return src[0, 0:rows], middle, src[1, 0:rows]

    @pl.when(me == 0)
    def _():
        for buf in (fr.at[0], fr.at[1], hr.at[0], hr.at[1], tr):
            buf[0] = jnp.zeros(buf.shape[1:], F32)

    @pl.when(me == n - 1)
    def _():
        for buf in (fr.at[0], fr.at[1], hr.at[0], hr.at[1], tr):
            buf[1] = jnp.zeros(buf.shape[1:], F32)

    terms = rhs_ref.shape[0]
    nodes = rhs_ref.shape[1]
    inp[...] = jnp.zeros_like(inp)
    inp[0:terms] = rhs_ref[...]
    inp[ROWS : ROWS + 8] = var_ref[...]
    inp[ROWS + 8 : ROWS + 9] = cap_ref[...]
    order = (
        lax.broadcasted_iota(jnp.int32, (nodes, nodes), 0) == codes_ref[0:1, 0:nodes]
    ).astype(F32).astype(BF16)
    h, m, l = split3(inp[...])
    moved = nn(h, order) + (nn(m, order) + nn(l, order))
    fieldb[...] = moved[:ROWS] * wide(scale_ref[0])
    lam[0:8] = moved[ROWS : ROWS + 8] * SPREAD
    lam[8:9] = jnp.ones((1, nodes), F32)
    lam[9:16] = jnp.zeros((7, nodes), F32)
    cap = moved[ROWS + 8 : ROWS + 9]

    pl.semaphore_wait(barrier, n - 1)

    def send_field(i, x):
        pack(fs.at[i], x[:, 0:128], x[:, 128:256], x[:, 256:384])
        send(*pair(fs.at[i], fr.at[i], i))

    send_field(0, fieldb[...])

    def couple_first():
        h, l = split2(fieldb[...])
        accb[...] = fieldb[...]

        def step(k, c):
            y = nn(coup_ref[k], h) + nn(coup_ref[k], l)
            ybuf[k] = y
            accb[...] += lam[pl.ds(k, 1)] * y
            return c

        lax.fori_loop(0, VARS, step, 0)
        gamb[...] = accb[...]

    couple_first()

    rowsc, rowse = wc.shape[0], base.shape[0]
    pick = (
        lax.broadcasted_iota(jnp.int32, (rowsc, rowse), 0) == codes_ref[0:1, 384 : 384 + rowse]
    ).astype(F32).astype(BF16)
    for i in range(4):
        base_copy(i).wait()

        def merge(j, c):
            cols = pl.ds(pl.multiple_of(i * chunk + j * 512, 512), 512)
            h, l = split2(base[:, cols])
            wc[:, cols] = nn(pick, h) + nn(pick, l)
            return c

        lax.fori_loop(0, chunk // 512, merge, 0)
    left8 = left_mask(8)

    def lay(j, c):
        cols = pl.ds(pl.multiple_of(j * 128, 128), 128)
        for t in range(6):
            even = wc[t * 16 : t * 16 + 8, cols]
            odd = wc[t * 16 + 8 : t * 16 + 16, cols]
            wf[pl.ds(t * 64 + 2 * j, 8, stride=nodes), :] = jnp.where(left8, even, swap(odd))
            wf[pl.ds(t * 64 + 2 * j + 1, 8, stride=nodes), :] = jnp.where(left8, swap(even), odd)
        return c

    lax.fori_loop(0, 32, lay, 0)
    for q in range(6):
        h, l = split2(wf[q * nodes : (q + 1) * nodes])
        whi[:, q * 128 : (q + 1) * 128] = h
        wlo[:, q * 128 : (q + 1) * 128] = l

    def three(a, b, bl, dot):
        h, l = split2(a)
        return dot(h, b) + (dot(l, b) + dot(h, bl))

    toward = three(lam[...], whi[...], wlo[...], nn)
    pack(ts, toward[:, 384:512], toward[:, 512:640], toward[:, 640:768])
    t_up = remote(ts.at[0], tr.at[1], 9, prev)
    t_down = remote(ts.at[1], tr.at[0], 8, nxt)

    def send_back(back, fwd):
        send(fwd, back)

    send_back(t_up, t_down)

    def flux_pair(i):
        to_prev = remote(hs.at[i, 0], hr.at[i, 1], 2 * (2 + i) + 1, prev)
        to_next = remote(hs.at[i, 1], hr.at[i, 0], 2 * (2 + i), nxt)
        return to_prev, to_next

    def send_flux(i):
        flux = three(gamb[...], whi[...], wlo[...], nn)
        pack(hs.at[i], flux[:, 384:512], flux[:, 512:640], flux[:, 640:768])
        to_prev, to_next = flux_pair(i)
        send(to_next, to_prev)
        qb[...] = -flux[:, 0:384]

    def neighbours(i, x):
        arrive(*pair(fs.at[i], fr.at[i], i))
        ext[:, 0:384] = x
        a, b, c = unpack(fr.at[i], ROWS)
        ext[:, 384:512] = a
        ext[:, 512:640] = b
        ext[:, 640:768] = c
        return three(ext[...], whi[...], wlo[...], nt)

    def flux_in(i):
        to_prev, to_next = flux_pair(i)
        arrive(to_next, to_prev)
        rows = ROWS
        left = left_mask(HALF)
        up, down = hr[i, 1, rows : rows + HALF], hr[i, 0, rows : rows + HALF]
        middle = jnp.concatenate(
            [jnp.where(left, up, swap(down)), jnp.where(left, swap(up), down)], axis=0
        )
        return jnp.concatenate([hr[i, 1, 0:rows], middle, hr[i, 0, 0:rows]], axis=1)

    def fold(x):
        x = x[:, 0:128] + x[:, 128:256] + x[:, 256:384]
        total = x[0:8]
        for i in range(1, ROWS // 8):
            total = total + x[8 * i : 8 * i + 8]
        return total

    def all_copy(i, off):
        peer = lax.rem(me + off, n)
        return pltpu.make_async_remote_copy(
            src_ref=allb.at[i, me], dst_ref=allb.at[i, me],
            send_sem=all_send.at[i], recv_sem=all_recv.at[i],
            device_id={"space": peer}, device_id_type=MESH,
        )

    def send_products(i, x, coupled, z):
        weight = wide(scale_ref[1])
        allb[i, me, 0:8] = fold(x * x * weight)
        allb[i, me, 8:16] = fold((x * coupled - 2.0 * gamb[...] * z) * weight)

        def go(off, c):
            all_copy(i, off).start()
            return c

        lax.fori_loop(1, n, go, 0)

    def products(i):
        others = allb.at[i, pl.ds(0, n - 1)]
        pltpu.make_async_copy(others, others, all_recv.at[i]).wait()
        pltpu.make_async_copy(others, others, all_send.at[i]).wait()
        total = allb[i, 0]
        for d in range(1, n):
            total = total + allb[i, d]
        return (
            jnp.sum(total[0:8], keepdims=True),
            jnp.sum(total[8:16], keepdims=True),
        )

    def couple_neighbours(z):
        h, l = split2(z)
        accb[...] = z

        def step(k, c):
            y = nn(coup_ref[k], h) + nn(coup_ref[k], l)
            accb[...] += lam[pl.ds(k, 1)] * y
            return c

        lax.fori_loop(0, VARS, step, 0)
        qb[...] -= accb[...]

    send_flux(0)
    z = neighbours(0, fieldb[...])
    ones = jnp.ones((16, 768), BF16)
    row_total = (nt(ones, whi[...]) + nt(ones, wlo[...]))[0:1]
    send_t = (t_down, t_up)
    arrive(*send_t)
    left = left_mask(8)
    up, down = tr[1, 16:24], tr[0, 16:24]
    middle = jnp.concatenate(
        [jnp.where(left, up, swap(down)), jnp.where(left, swap(up), down)], axis=0
    )
    came = jnp.concatenate([tr[1, 0:16], middle, tr[0, 0:16]], axis=1)
    dmode[...] = toward[:, 0:384] + came + row_total * lam[...]
    dmode[8:9] += cap
    cplb[...] = dmode[8:9] * fieldb[...]

    def join(k, c):
        cplb[...] += dmode[pl.ds(k, 1)] * ybuf[k]
        return c

    lax.fori_loop(0, VARS, join, 0)
    send_products(0, fieldb[...], cplb[...], z)
    couple_neighbours(z)
    image0 = qb[...] + cplb[...] - flux_in(0)
    norm0, product0 = products(0)
    step0 = norm0 / product0
    qb0 = image0
    r1b[...] = fieldb[...] - step0 * image0
    ext_q = ybuf
    send_field(1, r1b[...])

    h, l = split2(r1b[...])
    accb[...] = r1b[...]
    cplb[...] = dmode[8:9] * r1b[...]
    ext_q[0] = qb0

    def both(k, c):
        y = nn(coup_ref[k], h) + nn(coup_ref[k], l)
        accb[...] += lam[pl.ds(k, 1)] * y
        cplb[...] += dmode[pl.ds(k, 1)] * y
        return c

    lax.fori_loop(0, VARS, both, 0)
    gamb[...] = accb[...]
    send_flux(1)
    z = neighbours(1, r1b[...])
    send_products(1, r1b[...], cplb[...], z)
    couple_neighbours(z)
    norm1, product1 = products(1)
    ratio = norm1 / norm0
    step1 = norm1 / (product1 - ratio * norm1 / step0)

    def put_back(x):
        h, m, l = split3(x)
        y = nt(h, order) + (nt(m, order) + nt(l, order))
        return (y * wide(scale_ref[2]))[0:terms]

    x_ref[...] = put_back((step0 + step1 * ratio) * fieldb[...] + step1 * r1b[...])
    image1 = qb[...] + cplb[...] - flux_in(1)
    r_ref[...] = put_back(r1b[...] - step1 * (image1 + ratio * ext_q[0]))

    for i in range(2):
        sent(*pair(fs.at[i], fr.at[i], i))
        to_prev, to_next = flux_pair(i)
        sent(to_next, to_prev)
    sent(*send_t)


def shards(right_side, capacity, base_cond, var_field, block_cols, send_list):
    n = lax.axis_size("space")
    terms, nodes = right_side.shape
    blocks, slots, area = base_cond.shape
    width = nodes // blocks
    ups, downs = send_list[0, 0], send_list[0, 1]
    perm = jnp.concatenate([ups, downs[2:3], downs[0:2]])
    local = jnp.arange(blocks, dtype=jnp.int32)
    place = jnp.sum(
        jnp.where(perm[:, None] == local[None, :], local[:, None], 0), axis=0, dtype=jnp.int32
    )
    source = (perm[:, None] * width + jnp.arange(width, dtype=jnp.int32)[None, :]).reshape(1, nodes)
    columns = jnp.concatenate([local[:, None], block_cols], axis=1)
    inside = jnp.sum(
        jnp.where(columns[:, :, None] == local, place, 0), axis=2, dtype=jnp.int32
    )
    outside = jnp.where(columns < 9, columns, jnp.where(columns == 11, 9, columns + 1))
    where = jnp.where(columns < blocks, inside, outside)
    target = place[:, None] * 16 + (where % 2) * 8 + where // 2
    codes = jnp.concatenate([source, target.reshape(1, blocks * slots)], axis=1)
    codes = jnp.pad(codes, ((0, 0), (0, 640 - codes.shape[1])), constant_values=-1)
    coupling, scales = chaos_tables()
    vmem = pl.BlockSpec(memory_space=pltpu.VMEM)
    field = pltpu.VMEM((ROWS, nodes), F32)
    return pl.pallas_call(
        functools.partial(kernel, n),
        out_shape=(
            jax.ShapeDtypeStruct((terms, nodes), F32),
            jax.ShapeDtypeStruct((terms, nodes), F32),
        ),
        in_specs=[vmem] * 6 + [pl.BlockSpec(memory_space=pl.ANY)],
        out_specs=(vmem, vmem),
        scratch_shapes=[
            pltpu.VMEM((ROWS + 16, nodes), F32),
            pltpu.VMEM((blocks * slots, area), F32),
            pltpu.VMEM((blocks * 16, area), F32),
            pltpu.VMEM((8 * nodes, 128), F32),
            pltpu.VMEM((nodes, 2 * nodes), BF16),
            pltpu.VMEM((nodes, 2 * nodes), BF16),
            pltpu.VMEM((VARS, ROWS, nodes), F32),
            pltpu.VMEM((ROWS, 2 * nodes), F32),
            pltpu.VMEM((16, nodes), F32),
            pltpu.VMEM((16, nodes), F32),
            field, field, field, field, field, field,
            pltpu.VMEM((2, 2, MSG, 128), F32),
            pltpu.VMEM((2, 2, MSG, 128), F32),
            pltpu.VMEM((2, 2, MSG, 128), F32),
            pltpu.VMEM((2, 2, MSG, 128), F32),
            pltpu.VMEM((2, 24, 128), F32),
            pltpu.VMEM((2, 24, 128), F32),
            pltpu.VMEM((2, n, 16, 128), F32),
            pltpu.SemaphoreType.DMA((4,)),
            pltpu.SemaphoreType.DMA((10,)),
            pltpu.SemaphoreType.DMA((10,)),
            pltpu.SemaphoreType.DMA((2,)),
            pltpu.SemaphoreType.DMA((2,)),
        ],
        compiler_params=pltpu.CompilerParams(
            collective_id=0, has_side_effects=True, vmem_limit_bytes=48 * 1024 * 1024
        ),
        name="galerkin_cg",
    )(
        right_side, var_field, capacity.reshape(1, nodes), codes,
        jnp.asarray(coupling, BF16), jnp.asarray(scales), base_cond.reshape(blocks * slots, area),
    )


def solution(mesh):
    return jax.shard_map(
        shards,
        mesh=mesh,
        in_specs=(
            P(None, ("grp", "space")),
            P(("grp", "space")),
            P(("grp", "space"), None, None),
            P(None, ("grp", "space")),
            P(("grp", "space"), None),
            P(("grp", "space"), None, None),
        ),
        out_specs=(P(None, ("grp", "space")), P(None, ("grp", "space"))),
        check_vma=False,
    )
```

```python
import functools
import math

import jax
import jax.numpy as jnp
import numpy as np
from jax import lax
from jax.experimental import pallas as pl
from jax.experimental.pallas import tpu as pltpu
from jax.sharding import PartitionSpec as P

VARS = 8
ORDER = 3
ITERS = 2
SPREAD = 0.14
ROWS = 176
LOW, GAP, DEEP, LIVE = 45, 3, 48, 168
HALF = ROWS // 2
MSG = LIVE + HALF
MESH = pl.DeviceIdType.MESH
F32 = jnp.float32
BF16 = jnp.bfloat16


def chaos_tables():
    entries = []

    def grow(prefix, left):
        if len(prefix) == VARS:
            entries.append(tuple(prefix))
            return
        for degree in range(left + 1):
            grow(prefix + [degree], left - degree)

    grow([], ORDER)
    entries.sort(key=lambda m: (sum(m), tuple(-v for v in m)))
    lookup = {m: i if i < LOW else i + GAP for i, m in enumerate(entries)}
    coupling = np.zeros((768, 2 * ROWS), np.float32)
    expand = np.zeros((384, 16), np.float32)
    scale = np.ones((ROWS,), np.float64)
    for m, i in lookup.items():
        scale[i] = math.sqrt(math.prod(math.factorial(v) for v in m))
        held = [k for k in range(VARS) if m[k] > 0]
        for k in range(VARS):
            lowered = lookup.get(m[:k] + (m[k] - 1,) + m[k + 1 :])
            raised = lookup.get(m[:k] + (m[k] + 1,) + m[k + 1 :])
            for shift in (0, ROWS):
                if i < DEEP:
                    if lowered is not None:
                        coupling[DEEP * k + i, shift + lowered] = m[k]
                    coupling[DEEP * k + i, shift + raised] = 1.0
                elif m[k] > 0:
                    place = 120 * held.index(k) + i - DEEP
                    coupling[384 + place, shift + lowered] = m[k]
                    expand[place, k] = 1.0
    scales = np.stack([scale, 1.0 / scale**2, 1.0 / scale], 0)
    scales = np.broadcast_to(scales[:, :, None], (3, ROWS, 128)).astype(np.float32)
    return coupling, expand, scales


def split2(x):
    hi = x.astype(BF16)
    return hi, (x - hi.astype(F32)).astype(BF16)


def split3(x):
    hi = x.astype(BF16)
    rest = x - hi.astype(F32)
    mid = rest.astype(BF16)
    return hi, mid, (rest - mid.astype(F32)).astype(BF16)


def nn(a, b):
    return lax.dot_general(a, b, (((1,), (0,)), ((), ())), preferred_element_type=F32)


def nt(a, b):
    return lax.dot_general(a, b, (((1,), (1,)), ((), ())), preferred_element_type=F32)


def swap(x):
    return pltpu.roll(x, 64, 1)


def wide(x):
    return jnp.concatenate([x, x, x], axis=1)


def kernel(
    n,
    rhs_hbm, var_hbm, cap_hbm, cols_hbm, list_hbm, coup_hbm, expand_hbm, scale_hbm, base_hbm,
    x_ref, r_ref,
    rhs, var, capv, colv, lists, coup, expand, scale, base,
    inp, blk, wc, wf, whi, wlo, ybuf, xs, ext, lam, lamx, dmode, dmodex,
    fieldb, gamb, cplb, qb, r1b,
    fs, fr, hs, hr, ts, tr, allb,
    in_sem, base_sem, send_sem, recv_sem, all_send, all_recv,
):
    me = lax.axis_index("space")
    prev, nxt = lax.rem(me + n - 1, n), lax.rem(me + 1, n)
    chunk = base.shape[1] // 4

    ins = [
        pltpu.make_async_copy(src, dst, in_sem.at[i])
        for i, (src, dst) in enumerate(
            (
                (list_hbm, lists), (rhs_hbm, rhs), (var_hbm, var), (cap_hbm, capv),
                (cols_hbm, colv), (scale_hbm, scale), (coup_hbm, coup), (expand_hbm, expand),
            )
        )
    ]

    def base_copy(i):
        cols = pl.ds(i * chunk, chunk)
        return pltpu.make_async_copy(base_hbm.at[:, cols], base.at[:, cols], base_sem.at[i])

    for copy in ins:
        copy.start()
    for i in range(4):
        base_copy(i).start()

    barrier = pltpu.get_barrier_semaphore()

    def greet(i, c):
        pl.semaphore_signal(
            barrier, inc=1, device_id={"space": lax.rem(me + i, n)}, device_id_type=MESH
        )
        return c

    lax.fori_loop(1, n, greet, 0)

    def remote(src, dst, which, peer):
        return pltpu.make_async_remote_copy(
            src_ref=src, dst_ref=dst, send_sem=send_sem.at[which], recv_sem=recv_sem.at[which],
            device_id={"space": peer}, device_id_type=MESH,
        )

    def pair(src, dst, e):
        return remote(src.at[0], dst.at[0], 2 * e, nxt), remote(src.at[1], dst.at[1], 2 * e + 1, prev)

    def send(up, down):
        @pl.when(me < n - 1)
        def _():
            up.start()

        @pl.when(me > 0)
        def _():
            down.start()

    def arrive(up, down):
        @pl.when(me > 0)
        def _():
            up.wait_recv()

        @pl.when(me < n - 1)
        def _():
            down.wait_recv()

    def sent(up, down):
        @pl.when(me < n - 1)
        def _():
            up.wait_send()

        @pl.when(me > 0)
        def _():
            down.wait_send()

    def left_mask(rows):
        return lax.broadcasted_iota(jnp.int32, (rows, 128), 1) < 64

    def halves(left_of, right_of):
        return jnp.where(left_mask(left_of.shape[0]), left_of, right_of)

    def pack(first_dst, last_dst, first, middle, last):
        half = middle.shape[0] // 2
        rows = first_dst.shape[0] - half
        top, low = middle[:half], middle[half:]
        first_dst[0:rows] = first[:rows]
        first_dst[rows : rows + half] = halves(top, swap(low))
        last_dst[0:rows] = last[:rows]
        last_dst[rows : rows + half] = halves(swap(top), low)

    def unpack(first_src, last_src, half):
        rows = first_src.shape[0] - half
        a, b = first_src[rows : rows + half], last_src[rows : rows + half]
        middle = jnp.concatenate([halves(a, swap(b)), halves(swap(a), b)], axis=0)
        first, last = first_src[0:rows], last_src[0:rows]
        if rows < 2 * half:
            pad = jnp.zeros((2 * half - rows, 128), F32)
            first = jnp.concatenate([first, pad], axis=0)
            last = jnp.concatenate([last, pad], axis=0)
        return first, middle, last

    @pl.when(me == 0)
    def _():
        for buf in (fr.at[0, 0], fr.at[1, 0], hr.at[0, 0], hr.at[1, 0], tr.at[0]):
            buf[...] = jnp.zeros(buf.shape, F32)

    @pl.when(me == n - 1)
    def _():
        for buf in (fr.at[0, 1], fr.at[1, 1], hr.at[0, 1], hr.at[1, 1], tr.at[1]):
            buf[...] = jnp.zeros(buf.shape, F32)

    nodes = rhs.shape[1]
    terms = rhs.shape[0]
    inp[...] = jnp.zeros_like(inp)
    for copy in ins[:4]:
        copy.wait()
    perm = [lists[0, 0, 0], lists[0, 0, 1], lists[0, 0, 2], lists[0, 1, 2], lists[0, 1, 0], lists[0, 1, 1]]
    place = []
    for r in range(6):
        at = jnp.int32(0)
        for t in range(1, 6):
            at = jnp.where(perm[t] == r, jnp.int32(t), at)
        place.append(at)
    inp[0:LOW] = rhs[0:LOW]
    inp[DEEP:LIVE] = rhs[LOW:terms]
    inp[ROWS : ROWS + 8] = var[...]
    inp[ROWS + 8 : ROWS + 9] = capv[...].reshape(1, nodes)

    def reorder(tiles, index):
        rows = tiles[0].shape[0]
        for t in range(3):
            other = swap(tiles[t])
            blk[2 * t, 0:rows] = halves(tiles[t], other)
            blk[2 * t + 1, 0:rows] = halves(other, tiles[t])
        return [halves(blk[index[2 * t], 0:rows], blk[index[2 * t + 1], 0:rows]) for t in range(3)]

    moved = reorder([inp[:, t * 128 : (t + 1) * 128] for t in range(3)], perm)
    ins[5].wait()
    for t in range(3):
        cols = slice(t * 128, (t + 1) * 128)
        fieldb[:, cols] = moved[t][:ROWS] * scale[0]
        lam[0:8, cols] = moved[t][ROWS : ROWS + 8] * SPREAD
        dmode[0:16, cols] = moved[t][ROWS : ROWS + 16]
    lam[8:9] = jnp.ones((1, nodes), F32)
    lam[9:16] = jnp.zeros((7, nodes), F32)
    cap = dmode[8:9]

    pl.semaphore_wait(barrier, n - 1)

    def send_field(i, x):
        pack(fs.at[i, 0], fs.at[i, 1], x[:, 0:128], x[:, 128:256], x[:, 256:384])
        send(*pair(fs.at[i], fr.at[i], i))

    send_field(0, fieldb[...])

    def split_to(dst, x, cols=slice(None)):
        h, l = split2(x)
        dst[0:ROWS, cols] = h
        dst[ROWS : 2 * ROWS, cols] = l

    def spread(x):
        split_to(xs, x)
        ybuf[...] = nn(coup[...], xs[...])

    def joined(x, w, wx):
        top = w[8:9] * x[0:DEEP]
        for k in range(VARS):
            top = top + w[k : k + 1] * ybuf[DEEP * k : DEEP * (k + 1)]
        low = w[8:9] * x[DEEP:LIVE]
        for s in range(3):
            low = low + wx[120 * s : 120 * s + 120] * ybuf[384 + 120 * s : 504 + 120 * s]
        return jnp.concatenate([top, low, jnp.zeros((ROWS - LIVE, nodes), F32)], axis=0)

    def expanded(w):
        h, m, l = split3(w[...])
        e = expand[...]
        return nn(e, h) + (nn(e, m) + nn(e, l))

    ins[6].wait()
    ins[7].wait()
    lamx[...] = expanded(lam)
    spread(fieldb[...])
    gamb[...] = joined(fieldb[...], lam, lamx)

    rowsc, rowse = wc.shape[0], base.shape[0]
    ins[4].wait()
    slots = rowse // 6
    lane = lax.broadcasted_iota(jnp.int32, (1, rowse), 1)
    owner = jnp.zeros((1, rowse), jnp.int32)
    for j in range(1, 6):
        owner = owner + jnp.where(lane >= slots * j, 1, 0)
    slot = lane - slots * owner
    repeat = lax.broadcasted_iota(jnp.int32, (slots - 1, rowse), 0) == slot - 1
    given = nn(colv[...].astype(F32).astype(BF16), repeat.astype(F32).astype(BF16))
    given = jnp.where(lax.broadcasted_iota(jnp.int32, given.shape, 0) == owner, given, 0.0)
    column = jnp.sum(given, axis=0, keepdims=True).astype(jnp.int32)
    column = jnp.where(slot == 0, owner, column)
    where = jnp.where(column < 9, column, jnp.where(column == 11, 9, column + 1))
    row = jnp.zeros((1, rowse), jnp.int32)
    for j in range(6):
        where = jnp.where(column == j, place[j], where)
        row = jnp.where(owner == j, place[j], row)
    target = row * 16 + (where & 1) * 8 + (where >> 1)
    pick = (
        lax.broadcasted_iota(jnp.int32, (rowsc, rowse), 0) == target
    ).astype(F32).astype(BF16)
    for i in range(4):
        base_copy(i).wait()
        for j in range(2):
            cols = slice(i * chunk + j * 512, i * chunk + j * 512 + 512)
            h, l = split2(base[:, cols])
            wc[:, cols] = nn(pick, h) + nn(pick, l)

    def lay(j, c):
        cols = pl.ds(pl.multiple_of(j * 128, 128), 128)
        for t in range(6):
            even = wc[t * 16 : t * 16 + 8, cols]
            odd = wc[t * 16 + 8 : t * 16 + 16, cols]
            wf[pl.ds(t * 64 + 2 * j, 8, stride=nodes), :] = halves(even, swap(odd))
            wf[pl.ds(t * 64 + 2 * j + 1, 8, stride=nodes), :] = halves(swap(even), odd)
        return c

    lax.fori_loop(0, 32, lay, 0, unroll=4)
    for q in range(6):
        h, l = split2(wf[q * nodes : (q + 1) * nodes])
        whi[:, q * 128 : (q + 1) * 128] = h
        wlo[:, q * 128 : (q + 1) * 128] = l

    h, l = split2(lam[...])
    toward = nn(h, whi[...]) + (nn(l, whi[...]) + nn(h, wlo[...]))
    pack(ts.at[0], ts.at[1], toward[:, 384:512], toward[:, 512:640], toward[:, 640:768])
    t_pair = (remote(ts.at[1], tr.at[0], 8, nxt), remote(ts.at[0], tr.at[1], 9, prev))
    send(*t_pair)

    def edges(src, dot):
        both = dot(src[...], whi[...])
        return both[0:ROWS] + both[ROWS : 2 * ROWS] + dot(src[0:ROWS], wlo[...])

    def flux_pair(i):
        to_prev = remote(hs.at[i, 0], hr.at[i, 1], 2 * (2 + i) + 1, prev)
        to_next = remote(hs.at[i, 1], hr.at[i, 0], 2 * (2 + i), nxt)
        return to_next, to_prev

    def send_flux(i):
        split_to(xs, gamb[...])
        flux = edges(xs, nn)
        pack(hs.at[i, 0], hs.at[i, 1], flux[:, 384:512], flux[:, 512:640], flux[:, 640:768])
        send(*flux_pair(i))
        qb[...] = -flux[:, 0:384]

    def neighbours(i, x):
        split_to(ext, x, slice(0, 384))
        arrive(*pair(fs.at[i], fr.at[i], i))
        for t, tile in enumerate(unpack(fr.at[i, 0], fr.at[i, 1], HALF)):
            split_to(ext, tile, slice(384 + t * 128, 512 + t * 128))
        return edges(ext, nt)

    def flux_in(i):
        arrive(*flux_pair(i))
        return jnp.concatenate(unpack(hr.at[i, 1], hr.at[i, 0], HALF), axis=1)

    def fold(x):
        x = x[:, 0:128] + x[:, 128:256] + x[:, 256:384]
        total = x[0:8]
        for i in range(1, ROWS // 8):
            total = total + x[8 * i : 8 * i + 8]
        return total

    def all_copy(i, off):
        return pltpu.make_async_remote_copy(
            src_ref=allb.at[i, me], dst_ref=allb.at[i, me],
            send_sem=all_send.at[i], recv_sem=all_recv.at[i],
            device_id={"space": lax.rem(me + off, n)}, device_id_type=MESH,
        )

    def send_products(i, x, coupled, z):
        weight = wide(scale[1])
        allb[i, me, 0:8] = fold(x * x * weight)
        allb[i, me, 8:16] = fold((x * coupled - 2.0 * gamb[...] * z) * weight)

        def go(off, c):
            all_copy(i, off).start()
            return c

        lax.fori_loop(1, n, go, 0)

    def products(i):
        others = allb.at[i, pl.ds(0, n - 1)]
        pltpu.make_async_copy(others, others, all_recv.at[i]).wait()
        pltpu.make_async_copy(others, others, all_send.at[i]).wait()
        total = allb[i, 0]
        for d in range(1, n):
            total = total + allb[i, d]
        return jnp.sum(total[0:8], keepdims=True), jnp.sum(total[8:16], keepdims=True)

    def couple_neighbours(z):
        spread(z)
        qb[...] += cplb[...] - joined(z, lam, lamx)

    send_flux(0)
    ones = jnp.ones((16, 768), BF16)
    row_total = (nt(ones, whi[...]) + nt(ones, wlo[...]))[0:1]
    arrive(*t_pair)
    came = jnp.concatenate(unpack(tr.at[1], tr.at[0], 8), axis=1)
    dmode[...] = toward[:, 0:384] + came + row_total * lam[...] + jnp.where(
        lax.broadcasted_iota(jnp.int32, (16, nodes), 0) == 8, cap, 0.0
    )
    dmodex[...] = expanded(dmode)
    cplb[...] = joined(fieldb[...], dmode, dmodex)
    z = neighbours(0, fieldb[...])
    send_products(0, fieldb[...], cplb[...], z)
    couple_neighbours(z)
    image0 = qb[...] - flux_in(0)
    norm0, product0 = products(0)
    step0 = norm0 / product0
    r1b[...] = fieldb[...] - step0 * image0
    send_field(1, r1b[...])

    spread(r1b[...])
    gamb[...] = joined(r1b[...], lam, lamx)
    send_flux(1)
    cplb[...] = joined(r1b[...], dmode, dmodex)
    z = neighbours(1, r1b[...])
    send_products(1, r1b[...], cplb[...], z)
    couple_neighbours(z)

    def put_back(x):
        tiles = reorder([x[:, t * 128 : (t + 1) * 128] for t in range(3)], place)
        return jnp.concatenate([tile * scale[2] for tile in tiles], axis=1)

    def put_out(ref, y):
        ref[0:LOW] = y[0:LOW]
        ref[LOW:terms] = y[DEEP:LIVE]

    fieldb[...] = put_back(r1b[...])
    norm1, product1 = products(1)
    ratio = norm1 / norm0
    step1 = norm1 / (product1 - ratio * norm1 / step0)
    put_out(x_ref, (step0 + step1 * ratio) * inp[0:ROWS] + step1 * fieldb[...])
    gamb[...] = fieldb[...] - (step1 * ratio / step0) * (inp[0:ROWS] - fieldb[...])
    image1 = qb[...] - flux_in(1)
    put_out(r_ref, gamb[...] - step1 * put_back(image1))

    for i in range(2):
        sent(*pair(fs.at[i], fr.at[i], i))
        sent(*flux_pair(i))
    sent(*t_pair)


def shards(right_side, capacity, base_cond, var_field, block_cols, send_list):
    n = lax.axis_size("space")
    terms, nodes = right_side.shape
    blocks, slots, area = base_cond.shape
    coupling, expand, scales = chaos_tables()
    vmem = pl.BlockSpec(memory_space=pltpu.VMEM)
    field = pltpu.VMEM((ROWS, nodes), F32)
    small = pltpu.VMEM((16, nodes), F32)
    message = pltpu.VMEM((2, 2, MSG, 128), F32)
    return pl.pallas_call(
        functools.partial(kernel, n),
        out_shape=(
            jax.ShapeDtypeStruct((terms, nodes), F32),
            jax.ShapeDtypeStruct((terms, nodes), F32),
        ),
        in_specs=[pl.BlockSpec(memory_space=pl.ANY)] * 9,
        out_specs=(vmem, vmem),
        scratch_shapes=[
            pltpu.VMEM((terms, nodes), F32),
            pltpu.VMEM(var_field.shape, F32),
            pltpu.VMEM(capacity.shape, F32),
            pltpu.VMEM(block_cols.shape, jnp.int32),
            pltpu.SMEM(send_list.shape, jnp.int32),
            pltpu.VMEM(coupling.shape, BF16),
            pltpu.VMEM(expand.shape, BF16),
            pltpu.VMEM(scales.shape, F32),
            pltpu.VMEM((blocks * slots, area), F32),
            pltpu.VMEM((ROWS + 16, nodes), F32),
            pltpu.VMEM((blocks, ROWS + 16, 128), F32),
            pltpu.VMEM((blocks * 16, area), F32),
            pltpu.VMEM((8 * nodes, 128), F32),
            pltpu.VMEM((nodes, 2 * nodes), BF16),
            pltpu.VMEM((nodes, 2 * nodes), BF16),
            pltpu.VMEM((768, nodes), F32),
            pltpu.VMEM((2 * ROWS, nodes), BF16),
            pltpu.VMEM((2 * ROWS, 2 * nodes), BF16),
            small, pltpu.VMEM((384, nodes), F32), small, pltpu.VMEM((384, nodes), F32),
            field, field, field, field, field,
            message, message, message, message,
            pltpu.VMEM((2, 24, 128), F32),
            pltpu.VMEM((2, 24, 128), F32),
            pltpu.VMEM((2, n, 16, 128), F32),
            pltpu.SemaphoreType.DMA((8,)),
            pltpu.SemaphoreType.DMA((4,)),
            pltpu.SemaphoreType.DMA((10,)),
            pltpu.SemaphoreType.DMA((10,)),
            pltpu.SemaphoreType.DMA((2,)),
            pltpu.SemaphoreType.DMA((2,)),
        ],
        compiler_params=pltpu.CompilerParams(
            collective_id=0, has_side_effects=True, vmem_limit_bytes=60 * 1024 * 1024
        ),
        name="galerkin_cg",
    )(
        right_side, var_field, capacity, block_cols, send_list,
        jnp.asarray(coupling, BF16), jnp.asarray(expand, BF16), jnp.asarray(scales),
        base_cond.reshape(blocks * slots, area),
    )


def solution(mesh):
    return jax.shard_map(
        shards,
        mesh=mesh,
        in_specs=(
            P(None, ("grp", "space")),
            P(("grp", "space")),
            P(("grp", "space"), None, None),
            P(None, ("grp", "space")),
            P(("grp", "space"), None),
            P(("grp", "space"), None, None),
        ),
        out_specs=(P(None, ("grp", "space")), P(None, ("grp", "space"))),
        check_vma=False,
    )
```

```python
import functools
import math

import jax
import jax.numpy as jnp
import numpy as np
from jax import lax
from jax.experimental import pallas as pl
from jax.experimental.pallas import tpu as pltpu
from jax.sharding import PartitionSpec as P

VARS = 8
ORDER = 3
ITERS = 2
SPREAD = 0.14
ROWS = 176
LOW, GAP, DEEP, LIVE = 45, 3, 48, 168
HALF = ROWS // 2
MSG = LIVE + HALF
MESH = pl.DeviceIdType.MESH
F32 = jnp.float32
BF16 = jnp.bfloat16


def chaos_tables():
    entries = []

    def grow(prefix, left):
        if len(prefix) == VARS:
            entries.append(tuple(prefix))
            return
        for degree in range(left + 1):
            grow(prefix + [degree], left - degree)

    grow([], ORDER)
    entries.sort(key=lambda m: (sum(m), tuple(-v for v in m)))
    lookup = {m: i if i < LOW else i + GAP for i, m in enumerate(entries)}
    coupling = np.zeros((768, 2 * ROWS), np.float32)
    expand = np.zeros((384, 16), np.float32)
    scale = np.ones((ROWS,), np.float64)
    for m, i in lookup.items():
        scale[i] = math.sqrt(math.prod(math.factorial(v) for v in m))
        held = [k for k in range(VARS) if m[k] > 0]
        for k in range(VARS):
            lowered = lookup.get(m[:k] + (m[k] - 1,) + m[k + 1 :])
            raised = lookup.get(m[:k] + (m[k] + 1,) + m[k + 1 :])
            for shift in (0, ROWS):
                if i < DEEP:
                    if lowered is not None:
                        coupling[DEEP * k + i, shift + lowered] = m[k]
                    coupling[DEEP * k + i, shift + raised] = 1.0
                elif m[k] > 0:
                    place = 120 * held.index(k) + i - DEEP
                    coupling[384 + place, shift + lowered] = m[k]
                    expand[place, k] = 1.0
    scales = np.stack([scale, 1.0 / scale**2, 1.0 / scale], 0)
    scales = np.broadcast_to(scales[:, :, None], (3, ROWS, 128)).astype(np.float32)
    return coupling, expand, scales


def split2(x):
    hi = x.astype(BF16)
    return hi, (x - hi.astype(F32)).astype(BF16)


def split3(x):
    hi = x.astype(BF16)
    rest = x - hi.astype(F32)
    mid = rest.astype(BF16)
    return hi, mid, (rest - mid.astype(F32)).astype(BF16)


def nn(a, b):
    return lax.dot_general(a, b, (((1,), (0,)), ((), ())), preferred_element_type=F32)


def nt(a, b):
    return lax.dot_general(a, b, (((1,), (1,)), ((), ())), preferred_element_type=F32)


def swap(x):
    return pltpu.roll(x, 64, 1)


def wide(x):
    return jnp.concatenate([x, x, x], axis=1)


def kernel(
    n,
    rhs_hbm, var_hbm, cap_hbm, cols_hbm, list_hbm, coup_hbm, expand_hbm, scale_hbm, base_hbm,
    x_ref, r_ref,
    rhs, var, capv, colv, lists, coup, expand, scale, base,
    inp, blk, wc, wf, whi, wlo, ybuf, xs, ext, lam, lamx, dmode, dmodex, caps,
    fieldb, gamb, cplb, zb, imageb, gamq, cplq, qb, r1b,
    fs, fr, hs, hr, ts, tr, allb,
    in_sem, base_sem, send_sem, recv_sem, all_send, all_recv,
):
    me = lax.axis_index("space")
    prev, nxt = lax.rem(me + n - 1, n), lax.rem(me + 1, n)
    chunk = base.shape[1] // 4

    ins = [
        pltpu.make_async_copy(src, dst, in_sem.at[i])
        for i, (src, dst) in enumerate(
            (
                (list_hbm, lists), (rhs_hbm, rhs), (var_hbm, var), (cap_hbm, capv),
                (cols_hbm, colv), (scale_hbm, scale), (coup_hbm, coup), (expand_hbm, expand),
            )
        )
    ]

    def base_copy(i):
        cols = pl.ds(i * chunk, chunk)
        return pltpu.make_async_copy(base_hbm.at[:, cols], base.at[:, cols], base_sem.at[i])

    for copy in ins:
        copy.start()
    for i in range(4):
        base_copy(i).start()

    barrier = pltpu.get_barrier_semaphore()

    def greet(i, c):
        pl.semaphore_signal(
            barrier, inc=1, device_id={"space": lax.rem(me + i, n)}, device_id_type=MESH
        )
        return c

    lax.fori_loop(1, n, greet, 0)

    def remote(src, dst, which, peer):
        return pltpu.make_async_remote_copy(
            src_ref=src, dst_ref=dst, send_sem=send_sem.at[which], recv_sem=recv_sem.at[which],
            device_id={"space": peer}, device_id_type=MESH,
        )

    def pair(src, dst, e):
        return remote(src.at[0], dst.at[0], 2 * e, nxt), remote(src.at[1], dst.at[1], 2 * e + 1, prev)

    def send(up, down):
        @pl.when(me < n - 1)
        def _():
            up.start()

        @pl.when(me > 0)
        def _():
            down.start()

    def arrive(up, down):
        @pl.when(me > 0)
        def _():
            up.wait_recv()

        @pl.when(me < n - 1)
        def _():
            down.wait_recv()

    def sent(up, down):
        @pl.when(me < n - 1)
        def _():
            up.wait_send()

        @pl.when(me > 0)
        def _():
            down.wait_send()

    def left_mask(rows):
        return lax.broadcasted_iota(jnp.int32, (rows, 128), 1) < 64

    def halves(left_of, right_of):
        return jnp.where(left_mask(left_of.shape[0]), left_of, right_of)

    def pack(first_dst, last_dst, first, middle, last):
        half = middle.shape[0] // 2
        rows = first_dst.shape[0] - half
        top, low = middle[:half], middle[half:]
        first_dst[0:rows] = first[:rows]
        first_dst[rows : rows + half] = halves(top, swap(low))
        last_dst[0:rows] = last[:rows]
        last_dst[rows : rows + half] = halves(swap(top), low)

    def unpack(first_src, last_src, half):
        rows = first_src.shape[0] - half
        a, b = first_src[rows : rows + half], last_src[rows : rows + half]
        middle = jnp.concatenate([halves(a, swap(b)), halves(swap(a), b)], axis=0)
        first, last = first_src[0:rows], last_src[0:rows]
        if rows < 2 * half:
            pad = jnp.zeros((2 * half - rows, 128), F32)
            first = jnp.concatenate([first, pad], axis=0)
            last = jnp.concatenate([last, pad], axis=0)
        return first, middle, last

    @pl.when(me == 0)
    def _():
        for buf in (fr.at[0, 0], fr.at[1, 0], hr.at[0, 0], hr.at[1, 0], tr.at[0]):
            buf[...] = jnp.zeros(buf.shape, F32)

    @pl.when(me == n - 1)
    def _():
        for buf in (fr.at[0, 1], fr.at[1, 1], hr.at[0, 1], hr.at[1, 1], tr.at[1]):
            buf[...] = jnp.zeros(buf.shape, F32)

    nodes = rhs.shape[1]
    terms = rhs.shape[0]
    inp[...] = jnp.zeros_like(inp)
    for copy in ins[:4]:
        copy.wait()
    perm = [lists[0, 0, 0], lists[0, 0, 1], lists[0, 0, 2], lists[0, 1, 2], lists[0, 1, 0], lists[0, 1, 1]]
    place = []
    for r in range(6):
        at = jnp.int32(0)
        for t in range(1, 6):
            at = jnp.where(perm[t] == r, jnp.int32(t), at)
        place.append(at)
    inp[0:LOW] = rhs[0:LOW]
    inp[DEEP:LIVE] = rhs[LOW:terms]
    inp[ROWS : ROWS + 8] = var[...]
    inp[ROWS + 8 : ROWS + 9] = capv[...].reshape(1, nodes)

    def reorder(tiles, index):
        rows = tiles[0].shape[0]
        for t in range(3):
            other = swap(tiles[t])
            blk[2 * t, 0:rows] = halves(tiles[t], other)
            blk[2 * t + 1, 0:rows] = halves(other, tiles[t])
        return [halves(blk[index[2 * t], 0:rows], blk[index[2 * t + 1], 0:rows]) for t in range(3)]

    moved = reorder([inp[:, t * 128 : (t + 1) * 128] for t in range(3)], perm)
    ins[5].wait()
    for t in range(3):
        cols = slice(t * 128, (t + 1) * 128)
        fieldb[:, cols] = moved[t][:ROWS] * scale[0]
        lam[0:8, cols] = moved[t][ROWS : ROWS + 8] * SPREAD
        caps[0:8, cols] = moved[t][ROWS + 8 : ROWS + 16]
    lam[8:9] = jnp.ones((1, nodes), F32)
    lam[9:16] = jnp.zeros((7, nodes), F32)
    cap = caps[0:1]

    pl.semaphore_wait(barrier, n - 1)

    def send_field(i, x):
        pack(fs.at[i, 0], fs.at[i, 1], x[:, 0:128], x[:, 128:256], x[:, 256:384])
        send(*pair(fs.at[i], fr.at[i], i))

    send_field(0, fieldb[...])

    def split_to(dst, x, cols=slice(None)):
        h, l = split2(x)
        dst[0:ROWS, cols] = h
        dst[ROWS : 2 * ROWS, cols] = l

    def spread(x):
        split_to(xs, x)
        ybuf[...] = nn(coup[...], xs[0 : 2 * ROWS])

    def joined(x, w, wx):
        top = w[8:9] * x[0:DEEP]
        for k in range(VARS):
            top = top + w[k : k + 1] * ybuf[DEEP * k : DEEP * (k + 1)]
        low = w[8:9] * x[DEEP:LIVE]
        for s in range(3):
            low = low + wx[120 * s : 120 * s + 120] * ybuf[384 + 120 * s : 504 + 120 * s]
        return jnp.concatenate([top, low, jnp.zeros((ROWS - LIVE, nodes), F32)], axis=0)

    def expanded(w):
        h, m, l = split3(w[...])
        e = expand[...]
        return nn(e, h) + (nn(e, m) + nn(e, l))

    ins[6].wait()
    ins[7].wait()
    lamx[...] = expanded(lam)
    spread(fieldb[...])
    gamb[...] = joined(fieldb[...], lam, lamx)

    rowsc, rowse = wc.shape[0], base.shape[0]
    ins[4].wait()
    slots = rowse // 6
    lane = lax.broadcasted_iota(jnp.int32, (1, rowse), 1)
    owner = jnp.zeros((1, rowse), jnp.int32)
    for j in range(1, 6):
        owner = owner + jnp.where(lane >= slots * j, 1, 0)
    slot = lane - slots * owner
    repeat = lax.broadcasted_iota(jnp.int32, (slots - 1, rowse), 0) == slot - 1
    given = nn(colv[...].astype(F32).astype(BF16), repeat.astype(F32).astype(BF16))
    given = jnp.where(lax.broadcasted_iota(jnp.int32, given.shape, 0) == owner, given, 0.0)
    column = jnp.sum(given, axis=0, keepdims=True).astype(jnp.int32)
    column = jnp.where(slot == 0, owner, column)
    where = jnp.where(column < 9, column, jnp.where(column == 11, 9, column + 1))
    row = jnp.zeros((1, rowse), jnp.int32)
    for j in range(6):
        where = jnp.where(column == j, place[j], where)
        row = jnp.where(owner == j, place[j], row)
    target = row * 16 + (where & 1) * 8 + (where >> 1)
    pick = (
        lax.broadcasted_iota(jnp.int32, (rowsc, rowse), 0) == target
    ).astype(F32).astype(BF16)
    for i in range(4):
        base_copy(i).wait()
        for j in range(2):
            cols = slice(i * chunk + j * 512, i * chunk + j * 512 + 512)
            h, l = split2(base[:, cols])
            wc[:, cols] = nn(pick, h) + nn(pick, l)

    def lay(j, c):
        cols = pl.ds(pl.multiple_of(j * 128, 128), 128)
        for t in range(6):
            even = wc[t * 16 : t * 16 + 8, cols]
            odd = wc[t * 16 + 8 : t * 16 + 16, cols]
            wf[pl.ds(t * 64 + 2 * j, 8, stride=nodes + 1), :] = halves(even, swap(odd))
            wf[pl.ds(t * 64 + 2 * j + 1, 8, stride=nodes + 1), :] = halves(swap(even), odd)
        return c

    lax.fori_loop(0, 32, lay, 0, unroll=4)
    for q in range(6):
        h, l = split2(wf[q * (nodes + 1) : q * (nodes + 1) + nodes])
        whi[:, q * 128 : (q + 1) * 128] = h
        wlo[:, q * 128 : (q + 1) * 128] = l

    t_pair = (remote(ts.at[1], tr.at[0], 8, nxt), remote(ts.at[0], tr.at[1], 9, prev))

    def edges(src, dot):
        both = dot(src[0 : 2 * ROWS], whi[...])
        return both[0:ROWS] + both[ROWS : 2 * ROWS] + dot(src[0:ROWS], wlo[...])

    def flux_pair(i):
        to_prev = remote(hs.at[i, 0], hr.at[i, 1], 2 * (2 + i) + 1, prev)
        to_next = remote(hs.at[i, 1], hr.at[i, 0], 2 * (2 + i), nxt)
        return to_next, to_prev

    def send_flux(i, gam):
        split_to(xs, gam[...])
        if i == 0:
            h, l = split2(lam[...])
            xs[2 * ROWS : 2 * ROWS + 16] = h
            xs[2 * ROWS + 16 : 2 * ROWS + 32] = l
            fine = nn(xs[...], whi[...])
            rest = jnp.concatenate([xs[0:ROWS], xs[2 * ROWS : 2 * ROWS + 16]], axis=0)
            rest = nn(rest, wlo[...])
            flux = fine[0:ROWS] + fine[ROWS : 2 * ROWS] + rest[0:ROWS]
            toward = fine[2 * ROWS : 2 * ROWS + 16] + fine[2 * ROWS + 16 :] + rest[ROWS:]
            pack(ts.at[0], ts.at[1], toward[:, 384:512], toward[:, 512:640], toward[:, 640:768])
            send(*t_pair)
            dmode[...] = toward[:, 0:384]
        else:
            flux = edges(xs, nn)
        pack(hs.at[i, 0], hs.at[i, 1], flux[:, 384:512], flux[:, 512:640], flux[:, 640:768])
        send(*flux_pair(i))
        qb[...] = -flux[:, 0:384]

    def neighbours(i, x):
        split_to(ext, x, slice(0, 384))
        arrive(*pair(fs.at[i], fr.at[i], i))
        for t, tile in enumerate(unpack(fr.at[i, 0], fr.at[i, 1], HALF)):
            split_to(ext, tile, slice(384 + t * 128, 512 + t * 128))
        return edges(ext, nt)

    def flux_in(i):
        arrive(*flux_pair(i))
        return jnp.concatenate(unpack(hr.at[i, 1], hr.at[i, 0], HALF), axis=1)

    def fold(x):
        x = x[:, 0:128] + x[:, 128:256] + x[:, 256:384]
        total = x[0:8]
        for i in range(1, ROWS // 8):
            total = total + x[8 * i : 8 * i + 8]
        return total

    def all_copy(i, off):
        return pltpu.make_async_remote_copy(
            src_ref=allb.at[i, me], dst_ref=allb.at[i, me],
            send_sem=all_send.at[i], recv_sem=all_recv.at[i],
            device_id={"space": lax.rem(me + off, n)}, device_id_type=MESH,
        )

    def send_products(i, x, coupled, gam, z):
        weight = wide(scale[1])
        norm = jnp.sum(fold(x * x * weight), axis=0, keepdims=True)
        product = jnp.sum(fold((x * coupled - 2.0 * gam * z) * weight), axis=0, keepdims=True)
        allb[i, me] = halves(norm + swap(norm), product + swap(product))

        def go(off, c):
            all_copy(i, off).start()
            return c

        lax.fori_loop(1, n, go, 0)

    def products(i):
        others = allb.at[i, pl.ds(0, n - 1)]
        pltpu.make_async_copy(others, others, all_recv.at[i]).wait()
        pltpu.make_async_copy(others, others, all_send.at[i]).wait()
        total = allb[i, 0]
        for d in range(1, n):
            total = total + allb[i, d]
        left = left_mask(1)
        return (
            jnp.sum(jnp.where(left, total, 0.0), keepdims=True),
            jnp.sum(jnp.where(left, 0.0, total), keepdims=True),
        )

    def couple_neighbours(z, coupled):
        spread(z)
        qb[...] += coupled - joined(z, lam, lamx)

    send_flux(0, gamb)
    ones = jnp.ones((16, 768), BF16)
    row_total = (nt(ones, whi[...]) + nt(ones, wlo[...]))[0:1]
    arrive(*t_pair)
    came = jnp.concatenate(unpack(tr.at[1], tr.at[0], 8), axis=1)
    dmode[...] += came + row_total * lam[...] + jnp.where(
        lax.broadcasted_iota(jnp.int32, (16, nodes), 0) == 8, cap, 0.0
    )
    dmodex[...] = expanded(dmode)
    cplb[...] = joined(fieldb[...], dmode, dmodex)
    zb[...] = neighbours(0, fieldb[...])
    send_products(0, fieldb[...], cplb[...], gamb[...], zb[...])
    couple_neighbours(zb[...], cplb[...])
    imageb[...] = qb[...] - flux_in(0)
    send_field(1, imageb[...])

    spread(imageb[...])
    gamq[...] = joined(imageb[...], lam, lamx)
    cplq[...] = joined(imageb[...], dmode, dmodex)
    send_flux(1, gamq)
    z = neighbours(1, imageb[...])
    norm0, product0 = products(0)
    step0 = norm0 / product0
    r1b[...] = fieldb[...] - step0 * imageb[...]
    send_products(
        1, r1b[...], cplb[...] - step0 * cplq[...], gamb[...] - step0 * gamq[...],
        zb[...] - step0 * z,
    )
    couple_neighbours(z, cplq[...])

    def put_back(x):
        tiles = reorder([x[:, t * 128 : (t + 1) * 128] for t in range(3)], place)
        return jnp.concatenate([tile * scale[2] for tile in tiles], axis=1)

    def put_out(ref, y):
        ref[0:LOW] = y[0:LOW]
        ref[LOW:terms] = y[DEEP:LIVE]

    fieldb[...] = put_back(r1b[...])
    norm1, product1 = products(1)
    ratio = norm1 / norm0
    step1 = norm1 / (product1 - ratio * norm1 / step0)
    put_out(x_ref, (step0 + step1 * ratio) * inp[0:ROWS] + step1 * fieldb[...])
    gamb[...] = fieldb[...] - (step1 * (1.0 + ratio) / step0) * (inp[0:ROWS] - fieldb[...])
    second = qb[...] - flux_in(1)
    put_out(r_ref, gamb[...] + (step1 * step0) * put_back(second))

    for i in range(2):
        sent(*pair(fs.at[i], fr.at[i], i))
        sent(*flux_pair(i))
    sent(*t_pair)


def shards(right_side, capacity, base_cond, var_field, block_cols, send_list):
    n = lax.axis_size("space")
    terms, nodes = right_side.shape
    blocks, slots, area = base_cond.shape
    coupling, expand, scales = chaos_tables()
    vmem = pl.BlockSpec(memory_space=pltpu.VMEM)
    field = pltpu.VMEM((ROWS, nodes), F32)
    small = pltpu.VMEM((16, nodes), F32)
    message = pltpu.VMEM((2, 2, MSG, 128), F32)
    return pl.pallas_call(
        functools.partial(kernel, n),
        out_shape=(
            pltpu.VMEM((terms, nodes), F32),
            pltpu.VMEM((terms, nodes), F32),
        ),
        in_specs=[pl.BlockSpec(memory_space=pltpu.HBM)] * 9,
        out_specs=(vmem, vmem),
        scratch_shapes=[
            pltpu.VMEM((terms, nodes), F32),
            pltpu.VMEM(var_field.shape, F32),
            pltpu.VMEM(capacity.shape, F32),
            pltpu.VMEM(block_cols.shape, jnp.int32),
            pltpu.SMEM(send_list.shape, jnp.int32),
            pltpu.VMEM(coupling.shape, BF16),
            pltpu.VMEM(expand.shape, BF16),
            pltpu.VMEM(scales.shape, F32),
            pltpu.VMEM((blocks * slots, area), F32),
            pltpu.VMEM((ROWS + 16, nodes), F32),
            pltpu.VMEM((blocks, ROWS + 16, 128), F32),
            pltpu.VMEM((blocks * 16, area), F32),
            pltpu.VMEM((8 * nodes + 8, 128), F32),
            pltpu.VMEM((nodes, 2 * nodes), BF16),
            pltpu.VMEM((nodes, 2 * nodes), BF16),
            pltpu.VMEM((768, nodes), F32),
            pltpu.VMEM((2 * ROWS + 32, nodes), BF16),
            pltpu.VMEM((2 * ROWS, 2 * nodes), BF16),
            small, pltpu.VMEM((384, nodes), F32), small, pltpu.VMEM((384, nodes), F32), small,
            field, field, field, field, field, field, field, field, field,
            message, message, message, message,
            pltpu.VMEM((2, 24, 128), F32),
            pltpu.VMEM((2, 24, 128), F32),
            pltpu.VMEM((2, n, 1, 128), F32),
            pltpu.SemaphoreType.DMA((8,)),
            pltpu.SemaphoreType.DMA((4,)),
            pltpu.SemaphoreType.DMA((10,)),
            pltpu.SemaphoreType.DMA((10,)),
            pltpu.SemaphoreType.DMA((2,)),
            pltpu.SemaphoreType.DMA((2,)),
        ],
        compiler_params=pltpu.CompilerParams(
            collective_id=0, has_side_effects=True, vmem_limit_bytes=60 * 1024 * 1024
        ),
        name="galerkin_cg",
    )(
        right_side, var_field, capacity, block_cols, send_list,
        jnp.asarray(coupling, BF16), jnp.asarray(expand, BF16), jnp.asarray(scales),
        base_cond.reshape(blocks * slots, area),
    )


def solution(mesh):
    return jax.shard_map(
        shards,
        mesh=mesh,
        in_specs=(
            P(None, ("grp", "space")),
            P(("grp", "space")),
            P(("grp", "space"), None, None),
            P(None, ("grp", "space")),
            P(("grp", "space"), None),
            P(("grp", "space"), None, None),
        ),
        out_specs=(P(None, ("grp", "space")), P(None, ("grp", "space"))),
        check_vma=False,
    )
```

```python
import functools
import math

import jax
import jax.numpy as jnp
import numpy as np
from jax import lax
from jax.experimental import pallas as pl
from jax.experimental.pallas import tpu as pltpu
from jax.sharding import PartitionSpec as P

VARS = 8
ORDER = 3
ITERS = 2
SPREAD = 0.14
ROWS = 176
LOW, GAP, DEEP, LIVE = 45, 3, 48, 168
HALF = ROWS // 2
MSG = LIVE + HALF
OWN, AWAY = slice(0, 384), slice(384, 768)
MESH = pl.DeviceIdType.MESH
F32 = jnp.float32
BF16 = jnp.bfloat16


def chaos_tables():
    entries = []

    def grow(prefix, left):
        if len(prefix) == VARS:
            entries.append(tuple(prefix))
            return
        for degree in range(left + 1):
            grow(prefix + [degree], left - degree)

    grow([], ORDER)
    entries.sort(key=lambda m: (sum(m), tuple(-v for v in m)))
    lookup = {m: i if i < LOW else i + GAP for i, m in enumerate(entries)}
    coupling = np.zeros((768, 2 * ROWS), np.float32)
    expand = np.zeros((384, 16), np.float32)
    scale = np.ones((ROWS,), np.float64)
    for m, i in lookup.items():
        scale[i] = math.sqrt(math.prod(math.factorial(v) for v in m))
        held = [k for k in range(VARS) if m[k] > 0]
        for k in range(VARS):
            lowered = lookup.get(m[:k] + (m[k] - 1,) + m[k + 1 :])
            raised = lookup.get(m[:k] + (m[k] + 1,) + m[k + 1 :])
            for shift in (0, ROWS):
                if i < DEEP:
                    if lowered is not None:
                        coupling[DEEP * k + i, shift + lowered] = m[k]
                    coupling[DEEP * k + i, shift + raised] = 1.0
                elif m[k] > 0:
                    place = 120 * held.index(k) + i - DEEP
                    coupling[384 + place, shift + lowered] = m[k]
                    expand[place, k] = 1.0
    scales = np.stack([scale, 1.0 / scale**2, 1.0 / scale], 0)
    scales = np.broadcast_to(scales[:, :, None], (3, ROWS, 128)).astype(np.float32)
    return coupling, expand, scales


def split2(x):
    hi = x.astype(BF16)
    return hi, (x - hi.astype(F32)).astype(BF16)


def split3(x):
    hi = x.astype(BF16)
    rest = x - hi.astype(F32)
    mid = rest.astype(BF16)
    return hi, mid, (rest - mid.astype(F32)).astype(BF16)


def nn(a, b):
    return lax.dot_general(a, b, (((1,), (0,)), ((), ())), preferred_element_type=F32)


def nt(a, b):
    return lax.dot_general(a, b, (((1,), (1,)), ((), ())), preferred_element_type=F32)


def swap(x):
    return pltpu.roll(x, 64, 1)


def wide(x):
    return jnp.concatenate([x, x, x], axis=1)


def kernel(
    n,
    rhs_hbm, var_hbm, cap_hbm, cols_hbm, list_hbm, coup_hbm, expand_hbm, scale_hbm, base_hbm,
    x_ref, r_ref,
    rhs, var, capv, colv, lists, coup, expand, scale, base,
    inp, blk, wc, wf, whi, wlo, ybuf, xs, ext, lam, lamx, dmode, dmodex, caps,
    fieldb, gamb, cplb, backb, imageb, cplq, backq, r1b,
    fs, fr, hs, hr, ts, tr, allb,
    in_sem, base_sem, send_sem, recv_sem, all_send, all_recv,
):
    me = lax.axis_index("space")
    prev, nxt = lax.rem(me + n - 1, n), lax.rem(me + 1, n)
    chunk = base.shape[1] // 4

    ins = [
        pltpu.make_async_copy(src, dst, in_sem.at[i])
        for i, (src, dst) in enumerate(
            (
                (list_hbm, lists), (rhs_hbm, rhs), (var_hbm, var), (cap_hbm, capv),
                (cols_hbm, colv), (scale_hbm, scale), (coup_hbm, coup), (expand_hbm, expand),
            )
        )
    ]

    def base_copy(i):
        cols = pl.ds(i * chunk, chunk)
        return pltpu.make_async_copy(base_hbm.at[:, cols], base.at[:, cols], base_sem.at[i])

    for copy in ins:
        copy.start()
    for i in range(4):
        base_copy(i).start()

    barrier = pltpu.get_barrier_semaphore()

    def greet(i, c):
        pl.semaphore_signal(
            barrier, inc=1, device_id={"space": lax.rem(me + i, n)}, device_id_type=MESH
        )
        return c

    lax.fori_loop(1, n, greet, 0)

    def remote(src, dst, which, peer):
        return pltpu.make_async_remote_copy(
            src_ref=src, dst_ref=dst, send_sem=send_sem.at[which], recv_sem=recv_sem.at[which],
            device_id={"space": peer}, device_id_type=MESH,
        )

    def pair(src, dst, e):
        return remote(src.at[0], dst.at[0], 2 * e, nxt), remote(src.at[1], dst.at[1], 2 * e + 1, prev)

    def send(up, down):
        @pl.when(me < n - 1)
        def _():
            up.start()

        @pl.when(me > 0)
        def _():
            down.start()

    def arrive(up, down):
        @pl.when(me > 0)
        def _():
            up.wait_recv()

        @pl.when(me < n - 1)
        def _():
            down.wait_recv()

    def sent(up, down):
        @pl.when(me < n - 1)
        def _():
            up.wait_send()

        @pl.when(me > 0)
        def _():
            down.wait_send()

    def left_mask(rows):
        return lax.broadcasted_iota(jnp.int32, (rows, 128), 1) < 64

    def halves(left_of, right_of):
        return jnp.where(left_mask(left_of.shape[0]), left_of, right_of)

    def pack(first_dst, last_dst, first, middle, last):
        half = middle.shape[0] // 2
        rows = first_dst.shape[0] - half
        top, low = middle[:half], middle[half:]
        first_dst[0:rows] = first[:rows]
        first_dst[rows : rows + half] = halves(top, swap(low))
        last_dst[0:rows] = last[:rows]
        last_dst[rows : rows + half] = halves(swap(top), low)

    def unpack(first_src, last_src, half):
        rows = first_src.shape[0] - half
        a, b = first_src[rows : rows + half], last_src[rows : rows + half]
        middle = jnp.concatenate([halves(a, swap(b)), halves(swap(a), b)], axis=0)
        first, last = first_src[0:rows], last_src[0:rows]
        if rows < 2 * half:
            pad = jnp.zeros((2 * half - rows, 128), F32)
            first = jnp.concatenate([first, pad], axis=0)
            last = jnp.concatenate([last, pad], axis=0)
        return first, middle, last

    @pl.when(me == 0)
    def _():
        for buf in (fr.at[0, 0], fr.at[1, 0], hr.at[0, 0], hr.at[1, 0], tr.at[0]):
            buf[...] = jnp.zeros(buf.shape, F32)

    @pl.when(me == n - 1)
    def _():
        for buf in (fr.at[0, 1], fr.at[1, 1], hr.at[0, 1], hr.at[1, 1], tr.at[1]):
            buf[...] = jnp.zeros(buf.shape, F32)

    nodes = rhs.shape[1]
    terms = rhs.shape[0]
    inp[...] = jnp.zeros_like(inp)
    for copy in ins[:4]:
        copy.wait()
    perm = [lists[0, 0, 0], lists[0, 0, 1], lists[0, 0, 2], lists[0, 1, 2], lists[0, 1, 0], lists[0, 1, 1]]
    place = []
    for r in range(6):
        at = jnp.int32(0)
        for t in range(1, 6):
            at = jnp.where(perm[t] == r, jnp.int32(t), at)
        place.append(at)
    inp[0:LOW] = rhs[0:LOW]
    inp[DEEP:LIVE] = rhs[LOW:terms]
    inp[ROWS : ROWS + 8] = var[...]
    inp[ROWS + 8 : ROWS + 9] = capv[...].reshape(1, nodes)

    def reorder(tiles, index):
        rows = tiles[0].shape[0]
        for t in range(3):
            other = swap(tiles[t])
            blk[2 * t, 0:rows] = halves(tiles[t], other)
            blk[2 * t + 1, 0:rows] = halves(other, tiles[t])
        return [halves(blk[index[2 * t], 0:rows], blk[index[2 * t + 1], 0:rows]) for t in range(3)]

    moved = reorder([inp[:, t * 128 : (t + 1) * 128] for t in range(3)], perm)
    ins[5].wait()
    for t in range(3):
        cols = slice(t * 128, (t + 1) * 128)
        fieldb[:, cols] = moved[t][:ROWS] * scale[0]
        lam[0:8, cols] = moved[t][ROWS : ROWS + 8] * SPREAD
        caps[0:8, cols] = moved[t][ROWS + 8 : ROWS + 16]
    lam[8:9] = jnp.ones((1, nodes), F32)
    lam[9:16] = jnp.zeros((7, nodes), F32)
    cap = caps[0:1]

    pl.semaphore_wait(barrier, n - 1)

    def send_field(i, x):
        pack(fs.at[i, 0], fs.at[i, 1], x[:, 0:128], x[:, 128:256], x[:, 256:384])
        send(*pair(fs.at[i], fr.at[i], i))

    send_field(0, fieldb[...])

    def split_to(dst, x, cols=slice(None)):
        h, l = split2(x)
        dst[0:ROWS, cols] = h
        dst[ROWS : 2 * ROWS, cols] = l

    def spread(x):
        ybuf[...] = nn(coup[...], x)

    def joined(x, w, wx):
        top = w[8:9] * x[0:DEEP]
        for k in range(VARS):
            top = top + w[k : k + 1] * ybuf[DEEP * k : DEEP * (k + 1)]
        low = w[8:9] * x[DEEP:LIVE]
        for s in range(3):
            low = low + wx[120 * s : 120 * s + 120] * ybuf[384 + 120 * s : 504 + 120 * s]
        return jnp.concatenate([top, low, jnp.zeros((ROWS - LIVE, nodes), F32)], axis=0)

    def expanded(w):
        h, m, l = split3(w[...])
        e = expand[...]
        return nn(e, h) + (nn(e, m) + nn(e, l))

    ins[6].wait()
    ins[7].wait()
    lamx[...] = expanded(lam)
    split_to(ext, fieldb[...], OWN)
    spread(ext[:, OWN])
    gamb[...] = joined(fieldb[...], lam, lamx)

    rowsc, rowse = wc.shape[0], base.shape[0]
    ins[4].wait()
    slots = rowse // 6
    lane = lax.broadcasted_iota(jnp.int32, (1, rowse), 1)
    owner = jnp.zeros((1, rowse), jnp.int32)
    for j in range(1, 6):
        owner = owner + jnp.where(lane >= slots * j, 1, 0)
    slot = lane - slots * owner
    repeat = lax.broadcasted_iota(jnp.int32, (slots - 1, rowse), 0) == slot - 1
    given = nn(colv[...].astype(F32).astype(BF16), repeat.astype(F32).astype(BF16))
    given = jnp.where(lax.broadcasted_iota(jnp.int32, given.shape, 0) == owner, given, 0.0)
    column = jnp.sum(given, axis=0, keepdims=True).astype(jnp.int32)
    column = jnp.where(slot == 0, owner, column)
    where = jnp.where(column < 9, column, jnp.where(column == 11, 9, column + 1))
    row = jnp.zeros((1, rowse), jnp.int32)
    for j in range(6):
        where = jnp.where(column == j, place[j], where)
        row = jnp.where(owner == j, place[j], row)
    target = row * 16 + (where & 1) * 8 + (where >> 1)
    pick = (
        lax.broadcasted_iota(jnp.int32, (rowsc, rowse), 0) == target
    ).astype(F32).astype(BF16)
    for i in range(4):
        base_copy(i).wait()
        for j in range(2):
            cols = slice(i * chunk + j * 512, i * chunk + j * 512 + 512)
            h, l = split2(base[:, cols])
            wc[:, cols] = nn(pick, h) + nn(pick, l)

    def lay(j, c):
        cols = pl.ds(pl.multiple_of(j * 128, 128), 128)
        for t in range(6):
            even = wc[t * 16 : t * 16 + 8, cols]
            odd = wc[t * 16 + 8 : t * 16 + 16, cols]
            wf[pl.ds(t * 64 + 2 * j, 8, stride=nodes + 1), :] = halves(even, swap(odd))
            wf[pl.ds(t * 64 + 2 * j + 1, 8, stride=nodes + 1), :] = halves(swap(even), odd)
        return c

    lax.fori_loop(0, 32, lay, 0, unroll=4)
    for q in (3, 4, 5, 0, 1, 2):
        h, l = split2(wf[q * (nodes + 1) : q * (nodes + 1) + nodes])
        whi[:, q * 128 : (q + 1) * 128] = h
        wlo[:, q * 128 : (q + 1) * 128] = l

    t_pair = (remote(ts.at[1], tr.at[0], 8, nxt), remote(ts.at[0], tr.at[1], 9, prev))

    def edges(src, cols, dot):
        left = src[0 : 2 * ROWS, cols] if dot is nt else src[0 : 2 * ROWS]
        both = dot(left, whi[:, cols])
        return both[0:ROWS] + both[ROWS : 2 * ROWS] + dot(left[0:ROWS], wlo[:, cols])

    def flux_pair(i):
        to_prev = remote(hs.at[i, 0], hr.at[i, 1], 2 * (2 + i) + 1, prev)
        to_next = remote(hs.at[i, 1], hr.at[i, 0], 2 * (2 + i), nxt)
        return to_next, to_prev

    def flux_and_weights(cols):
        fine = nn(xs[...], whi[:, cols])
        rest = jnp.concatenate([xs[0:ROWS], xs[2 * ROWS : 2 * ROWS + 16]], axis=0)
        rest = nn(rest, wlo[:, cols])
        return (
            fine[0:ROWS] + fine[ROWS : 2 * ROWS] + rest[0:ROWS],
            fine[2 * ROWS : 2 * ROWS + 16] + fine[2 * ROWS + 16 :] + rest[ROWS:],
        )

    def send_flux(i, flux):
        pack(hs.at[i, 0], hs.at[i, 1], flux[:, 0:128], flux[:, 128:256], flux[:, 256:384])
        send(*flux_pair(i))

    def outer(i):
        for t, tile in enumerate(unpack(fr.at[i, 0], fr.at[i, 1], HALF)):
            split_to(ext, tile, slice(384 + t * 128, 512 + t * 128))
        return edges(ext, AWAY, nt)

    def flux_in(i):
        arrive(*flux_pair(i))
        return jnp.concatenate(unpack(hr.at[i, 1], hr.at[i, 0], HALF), axis=1)

    def fold(x):
        total = x[0:8]
        for i in range(1, x.shape[0] // 8):
            total = total + x[8 * i : 8 * i + 8]
        return total

    def fold_wide(x):
        return fold(x[:, 0:128] + x[:, 128:256] + x[:, 256:384])

    def all_copy(i, off):
        return pltpu.make_async_remote_copy(
            src_ref=allb.at[i, me], dst_ref=allb.at[i, me],
            send_sem=all_send.at[i], recv_sem=all_recv.at[i],
            device_id={"space": lax.rem(me + off, n)}, device_id_type=MESH,
        )

    def send_products(i, x, rest, outside):
        weight = scale[1]
        packed = jnp.concatenate([weight[0:LIVE], halves(weight[:HALF], weight[HALF:])], axis=0)
        weight = wide(weight)
        norm = jnp.sum(fold_wide(x * x * weight), axis=0, keepdims=True)
        product = fold_wide(x * rest * weight) - 2.0 * fold(outside * packed)
        product = jnp.sum(product, axis=0, keepdims=True)
        allb[i, me] = halves(norm + swap(norm), product + swap(product))

        def go(off, c):
            all_copy(i, off).start()
            return c

        lax.fori_loop(1, n, go, 0)

    def products(i):
        others = allb.at[i, pl.ds(0, n - 1)]
        pltpu.make_async_copy(others, others, all_recv.at[i]).wait()
        pltpu.make_async_copy(others, others, all_send.at[i]).wait()
        total = allb[i, 0]
        for d in range(1, n):
            total = total + allb[i, d]
        left = left_mask(1)
        return (
            jnp.sum(jnp.where(left, total, 0.0), keepdims=True),
            jnp.sum(jnp.where(left, 0.0, total), keepdims=True),
        )

    split_to(xs, gamb[...])
    h, l = split2(lam[...])
    xs[2 * ROWS : 2 * ROWS + 16] = h
    xs[2 * ROWS + 16 : 2 * ROWS + 32] = l
    flux, toward = flux_and_weights(AWAY)
    pack(ts.at[0], ts.at[1], toward[:, 0:128], toward[:, 128:256], toward[:, 256:384])
    send(*t_pair)
    send_flux(0, flux)
    flux, toward = flux_and_weights(OWN)
    backb[...] = -flux
    inner = edges(ext, OWN, nt)
    ones = jnp.ones((16, 768), BF16)
    row_total = (nt(ones, whi[...]) + nt(ones, wlo[...]))[0:1]
    arrive(*t_pair)
    came = jnp.concatenate(unpack(tr.at[1], tr.at[0], 8), axis=1)
    dmode[...] = toward + came + row_total * lam[...] + jnp.where(
        lax.broadcasted_iota(jnp.int32, (16, nodes), 0) == 8, cap, 0.0
    )
    dmodex[...] = expanded(dmode)
    cplb[...] = joined(fieldb[...], dmode, dmodex)
    arrive(*pair(fs.at[0], fr.at[0], 0))
    send_products(
        0, fieldb[...], cplb[...] + 2.0 * backb[...], hs[0, 0] * fr[0, 0] + hs[0, 1] * fr[0, 1]
    )
    z = inner + outer(0)
    split_to(xs, z)
    spread(xs[0 : 2 * ROWS])
    imageb[...] = cplb[...] + backb[...] - joined(z, lam, lamx)
    imageb[...] -= flux_in(0)
    send_field(1, imageb[...])

    split_to(ext, imageb[...], OWN)
    spread(ext[:, OWN])
    split_to(xs, joined(imageb[...], lam, lamx))
    send_flux(1, edges(xs, AWAY, nn))
    cplq[...] = joined(imageb[...], dmode, dmodex)
    backq[...] = -edges(xs, OWN, nn)
    inner = edges(ext, OWN, nt)
    norm0, product0 = products(0)
    step0 = norm0 / product0
    r1b[...] = fieldb[...] - step0 * imageb[...]
    cplb[...] = (cplb[...] + 2.0 * backb[...]) - step0 * (cplq[...] + 2.0 * backq[...])
    arrive(*pair(fs.at[1], fr.at[1], 1))
    outside = (hs[0, 0] - step0 * hs[1, 0]) * (fr[0, 0] - step0 * fr[1, 0])
    outside += (hs[0, 1] - step0 * hs[1, 1]) * (fr[0, 1] - step0 * fr[1, 1])
    send_products(1, r1b[...], cplb[...], outside)
    z = inner + outer(1)
    split_to(xs, z)
    spread(xs[0 : 2 * ROWS])
    cplq[...] = cplq[...] + backq[...] - joined(z, lam, lamx)

    def put_back(x):
        tiles = reorder([x[:, t * 128 : (t + 1) * 128] for t in range(3)], place)
        return jnp.concatenate([tile * scale[2] for tile in tiles], axis=1)

    def put_out(ref, y):
        ref[0:LOW] = y[0:LOW]
        ref[LOW:terms] = y[DEEP:LIVE]

    fieldb[...] = put_back(r1b[...])
    norm1, product1 = products(1)
    ratio = norm1 / norm0
    step1 = norm1 / (product1 - ratio * norm1 / step0)
    put_out(x_ref, (step0 + step1 * ratio) * inp[0:ROWS] + step1 * fieldb[...])
    gamb[...] = fieldb[...] - (step1 * (1.0 + ratio) / step0) * (inp[0:ROWS] - fieldb[...])
    second = cplq[...] - flux_in(1)
    put_out(r_ref, gamb[...] + (step1 * step0) * put_back(second))

    for i in range(2):
        sent(*pair(fs.at[i], fr.at[i], i))
        sent(*flux_pair(i))
    sent(*t_pair)


def shards(right_side, capacity, base_cond, var_field, block_cols, send_list):
    n = lax.axis_size("space")
    terms, nodes = right_side.shape
    blocks, slots, area = base_cond.shape
    coupling, expand, scales = chaos_tables()
    vmem = pl.BlockSpec(memory_space=pltpu.VMEM)
    field = pltpu.VMEM((ROWS, nodes), F32)
    small = pltpu.VMEM((16, nodes), F32)
    message = pltpu.VMEM((2, 2, MSG, 128), F32)
    return pl.pallas_call(
        functools.partial(kernel, n),
        out_shape=(
            pltpu.VMEM((terms, nodes), F32),
            pltpu.VMEM((terms, nodes), F32),
        ),
        in_specs=[pl.BlockSpec(memory_space=pltpu.HBM)] * 9,
        out_specs=(vmem, vmem),
        scratch_shapes=[
            pltpu.VMEM((terms, nodes), F32),
            pltpu.VMEM(var_field.shape, F32),
            pltpu.VMEM(capacity.shape, F32),
            pltpu.VMEM(block_cols.shape, jnp.int32),
            pltpu.SMEM(send_list.shape, jnp.int32),
            pltpu.VMEM(coupling.shape, BF16),
            pltpu.VMEM(expand.shape, BF16),
            pltpu.VMEM(scales.shape, F32),
            pltpu.VMEM((blocks * slots, area), F32),
            pltpu.VMEM((ROWS + 16, nodes), F32),
            pltpu.VMEM((blocks, ROWS + 16, 128), F32),
            pltpu.VMEM((blocks * 16, area), F32),
            pltpu.VMEM((8 * nodes + 8, 128), F32),
            pltpu.VMEM((nodes, 2 * nodes), BF16),
            pltpu.VMEM((nodes, 2 * nodes), BF16),
            pltpu.VMEM((768, nodes), F32),
            pltpu.VMEM((2 * ROWS + 32, nodes), BF16),
            pltpu.VMEM((2 * ROWS, 2 * nodes), BF16),
            small, pltpu.VMEM((384, nodes), F32), small, pltpu.VMEM((384, nodes), F32), small,
            field, field, field, field, field, field, field, field,
            message, message, message, message,
            pltpu.VMEM((2, 24, 128), F32),
            pltpu.VMEM((2, 24, 128), F32),
            pltpu.VMEM((2, n, 1, 128), F32),
            pltpu.SemaphoreType.DMA((8,)),
            pltpu.SemaphoreType.DMA((4,)),
            pltpu.SemaphoreType.DMA((10,)),
            pltpu.SemaphoreType.DMA((10,)),
            pltpu.SemaphoreType.DMA((2,)),
            pltpu.SemaphoreType.DMA((2,)),
        ],
        compiler_params=pltpu.CompilerParams(
            collective_id=0, has_side_effects=True, vmem_limit_bytes=60 * 1024 * 1024
        ),
        name="galerkin_cg",
    )(
        right_side, var_field, capacity, block_cols, send_list,
        jnp.asarray(coupling, BF16), jnp.asarray(expand, BF16), jnp.asarray(scales),
        base_cond.reshape(blocks * slots, area),
    )


def solution(mesh):
    return jax.shard_map(
        shards,
        mesh=mesh,
        in_specs=(
            P(None, ("grp", "space")),
            P(("grp", "space")),
            P(("grp", "space"), None, None),
            P(None, ("grp", "space")),
            P(("grp", "space"), None),
            P(("grp", "space"), None, None),
        ),
        out_specs=(P(None, ("grp", "space")), P(None, ("grp", "space"))),
        check_vma=False,
    )
```

```python
import functools
import math

import jax
import jax.numpy as jnp
import numpy as np
from jax import lax
from jax.experimental import pallas as pl
from jax.experimental.pallas import tpu as pltpu
from jax.sharding import PartitionSpec as P

VARS = 8
ORDER = 3
ITERS = 2
SPREAD = 0.14
ROWS, EVEN, ODD, DEEP = 176, 40, 48, 56
PLACES = ((0, 1, 36), (1, 9, 48), (9, 45, 0), (45, 165, 56))
HALF = ROWS // 2
MSG = ROWS + HALF
OWN, AWAY = slice(0, 384), slice(384, 768)
MESH = pl.DeviceIdType.MESH
F32 = jnp.float32
BF16 = jnp.bfloat16


def chaos_tables():
    entries = []

    def grow(prefix, left):
        if len(prefix) == VARS:
            entries.append(tuple(prefix))
            return
        for degree in range(left + 1):
            grow(prefix + [degree], left - degree)

    grow([], ORDER)
    entries.sort(key=lambda m: (sum(m), tuple(-v for v in m)))
    lookup = {}
    for first, end, row in PLACES:
        for i in range(first, end):
            lookup[entries[i]] = row + i - first
    even = np.zeros((VARS * EVEN, 2 * (ROWS - ODD)), np.float32)
    odd = np.zeros((432, 2 * ODD), np.float32)
    expand = np.zeros((384, 16), np.float32)
    scale = np.ones((ROWS,), np.float64)
    for m, i in lookup.items():
        scale[i] = math.sqrt(math.prod(math.factorial(v) for v in m))
        held = [k for k in range(VARS) if m[k] > 0]
        for k in range(VARS):
            lowered = lookup.get(m[:k] + (m[k] - 1,) + m[k + 1 :])
            raised = lookup.get(m[:k] + (m[k] + 1,) + m[k + 1 :])
            for other, weight in ((lowered, m[k]), (raised, 1.0)):
                if other is None:
                    continue
                if i < EVEN:
                    even[EVEN * k + i, [other - ODD, ROWS - ODD + other - ODD]] = weight
                elif i < DEEP:
                    odd[8 * k + i - ODD, [other, ODD + other]] = weight
                else:
                    place = 120 * held.index(k) + i - DEEP
                    odd[64 + place, [other, ODD + other]] = weight
                    expand[place, k] = 1.0
    scales = np.stack([scale, 1.0 / scale**2, 1.0 / scale], 0)
    scales = np.broadcast_to(scales[:, :, None], (3, ROWS, 128)).astype(np.float32)
    return even, odd, expand, scales


def split2(x):
    hi = x.astype(BF16)
    return hi, (x - hi.astype(F32)).astype(BF16)


def split3(x):
    hi = x.astype(BF16)
    rest = x - hi.astype(F32)
    mid = rest.astype(BF16)
    return hi, mid, (rest - mid.astype(F32)).astype(BF16)


def nn(a, b):
    return lax.dot_general(a, b, (((1,), (0,)), ((), ())), preferred_element_type=F32)


def nt(a, b):
    return lax.dot_general(a, b, (((1,), (1,)), ((), ())), preferred_element_type=F32)


def swap(x):
    return pltpu.roll(x, 64, 1)


def wide(x):
    return jnp.concatenate([x, x, x], axis=1)


def kernel(
    n,
    rhs_hbm, var_hbm, cap_hbm, cols_hbm, list_hbm, even_hbm, odd_hbm, expand_hbm, scale_hbm, base_hbm,
    x_ref, r_ref,
    rhs, var, capv, colv, lists, even, odd, expand, scale, base,
    inp, blk, wc, wf, whi, wlo, ybuf, xs, ext, lam, lamx, dmode, dmodex, caps,
    fieldb, gamb, cplb, backb, imageb, cplq, backq, r1b,
    fs, fr, hs, hr, ts, tr, allb,
    in_sem, base_sem, send_sem, recv_sem, all_send, all_recv,
):
    me = lax.axis_index("space")
    prev, nxt = lax.rem(me + n - 1, n), lax.rem(me + 1, n)
    chunk = base.shape[1] // 4

    ins = [
        pltpu.make_async_copy(src, dst, in_sem.at[i])
        for i, (src, dst) in enumerate(
            (
                (list_hbm, lists), (rhs_hbm, rhs), (var_hbm, var), (cap_hbm, capv),
                (cols_hbm, colv), (scale_hbm, scale), (even_hbm, even), (odd_hbm, odd),
                (expand_hbm, expand),
            )
        )
    ]

    def base_copy(i):
        cols = pl.ds(i * chunk, chunk)
        return pltpu.make_async_copy(base_hbm.at[:, cols], base.at[:, cols], base_sem.at[i])

    for copy in ins:
        copy.start()
    for i in range(4):
        base_copy(i).start()

    barrier = pltpu.get_barrier_semaphore()

    def greet(i, c):
        pl.semaphore_signal(
            barrier, inc=1, device_id={"space": lax.rem(me + i, n)}, device_id_type=MESH
        )
        return c

    lax.fori_loop(1, n, greet, 0)

    def remote(src, dst, which, peer):
        return pltpu.make_async_remote_copy(
            src_ref=src, dst_ref=dst, send_sem=send_sem.at[which], recv_sem=recv_sem.at[which],
            device_id={"space": peer}, device_id_type=MESH,
        )

    def pair(src, dst, e):
        return remote(src.at[0], dst.at[0], 2 * e, nxt), remote(src.at[1], dst.at[1], 2 * e + 1, prev)

    def send(up, down):
        @pl.when(me < n - 1)
        def _():
            up.start()

        @pl.when(me > 0)
        def _():
            down.start()

    def arrive(up, down):
        @pl.when(me > 0)
        def _():
            up.wait_recv()

        @pl.when(me < n - 1)
        def _():
            down.wait_recv()

    def sent(up, down):
        @pl.when(me < n - 1)
        def _():
            up.wait_send()

        @pl.when(me > 0)
        def _():
            down.wait_send()

    def left_mask(rows):
        return lax.broadcasted_iota(jnp.int32, (rows, 128), 1) < 64

    def halves(left_of, right_of):
        return jnp.where(left_mask(left_of.shape[0]), left_of, right_of)

    def pack(first_dst, last_dst, first, middle, last):
        half = middle.shape[0] // 2
        rows = first_dst.shape[0] - half
        top, low = middle[:half], middle[half:]
        first_dst[0:rows] = first[:rows]
        first_dst[rows : rows + half] = halves(top, swap(low))
        last_dst[0:rows] = last[:rows]
        last_dst[rows : rows + half] = halves(swap(top), low)

    def unpack(first_src, last_src, half):
        rows = first_src.shape[0] - half
        a, b = first_src[rows : rows + half], last_src[rows : rows + half]
        middle = jnp.concatenate([halves(a, swap(b)), halves(swap(a), b)], axis=0)
        first, last = first_src[0:rows], last_src[0:rows]
        if rows < 2 * half:
            pad = jnp.zeros((2 * half - rows, 128), F32)
            first = jnp.concatenate([first, pad], axis=0)
            last = jnp.concatenate([last, pad], axis=0)
        return first, middle, last

    @pl.when(me == 0)
    def _():
        for buf in (fr.at[0, 0], fr.at[1, 0], hr.at[0, 0], hr.at[1, 0], tr.at[0]):
            buf[...] = jnp.zeros(buf.shape, F32)

    @pl.when(me == n - 1)
    def _():
        for buf in (fr.at[0, 1], fr.at[1, 1], hr.at[0, 1], hr.at[1, 1], tr.at[1]):
            buf[...] = jnp.zeros(buf.shape, F32)

    nodes = rhs.shape[1]
    terms = rhs.shape[0]
    inp[...] = jnp.zeros_like(inp)
    for copy in ins[:4]:
        copy.wait()
    perm = [lists[0, 0, 0], lists[0, 0, 1], lists[0, 0, 2], lists[0, 1, 2], lists[0, 1, 0], lists[0, 1, 1]]
    place = []
    for r in range(6):
        at = jnp.int32(0)
        for t in range(1, 6):
            at = jnp.where(perm[t] == r, jnp.int32(t), at)
        place.append(at)
    for first, end, row in PLACES:
        inp[row : row + end - first] = rhs[first:end]
    inp[ROWS : ROWS + 8] = var[...]
    inp[ROWS + 8 : ROWS + 9] = capv[...].reshape(1, nodes)

    def reorder(tiles, index):
        rows = tiles[0].shape[0]
        for t in range(3):
            other = swap(tiles[t])
            blk[2 * t, 0:rows] = halves(tiles[t], other)
            blk[2 * t + 1, 0:rows] = halves(other, tiles[t])
        return [halves(blk[index[2 * t], 0:rows], blk[index[2 * t + 1], 0:rows]) for t in range(3)]

    moved = reorder([inp[:, t * 128 : (t + 1) * 128] for t in range(3)], perm)
    ins[5].wait()
    for t in range(3):
        cols = slice(t * 128, (t + 1) * 128)
        fieldb[:, cols] = moved[t][:ROWS] * scale[0]
        lam[0:8, cols] = moved[t][ROWS : ROWS + 8] * SPREAD
        caps[0:8, cols] = moved[t][ROWS + 8 : ROWS + 16]
    lam[8:9] = jnp.ones((1, nodes), F32)
    lam[9:16] = jnp.zeros((7, nodes), F32)
    cap = caps[0:1]

    pl.semaphore_wait(barrier, n - 1)

    def send_field(i, x):
        pack(fs.at[i, 0], fs.at[i, 1], x[:, 0:128], x[:, 128:256], x[:, 256:384])
        send(*pair(fs.at[i], fr.at[i], i))

    send_field(0, fieldb[...])

    def split_to(dst, x, cols=slice(None)):
        h, l = split2(x)
        dst[0:ROWS, cols] = h
        dst[ROWS : 2 * ROWS, cols] = l

    def spread(src):
        cols = OWN
        up = jnp.concatenate([src[ODD:ROWS, cols], src[ROWS + ODD : 2 * ROWS, cols]], axis=0)
        down = jnp.concatenate([src[0:ODD, cols], src[ROWS : ROWS + ODD, cols]], axis=0)
        ybuf[0 : VARS * EVEN] = nn(even[...], up)
        ybuf[VARS * EVEN :] = nn(odd[...], down)

    def joined(x, w, wx):
        top = w[8:9] * x[0:EVEN]
        one = w[8:9] * x[ODD:DEEP]
        low = w[8:9] * x[DEEP:ROWS]
        ones_at = VARS * EVEN
        for k in range(VARS):
            top = top + w[k : k + 1] * ybuf[EVEN * k : EVEN * (k + 1)]
            one = one + w[k : k + 1] * ybuf[ones_at + 8 * k : ones_at + 8 * (k + 1)]
        deep_at = ones_at + 64
        for s in range(3):
            low = low + wx[120 * s : 120 * s + 120] * ybuf[deep_at + 120 * s : deep_at + 120 * s + 120]
        return jnp.concatenate([top, jnp.zeros((ODD - EVEN, nodes), F32), one, low], axis=0)

    def expanded(w):
        h, m, l = split3(w[...])
        e = expand[...]
        return nn(e, h) + (nn(e, m) + nn(e, l))

    ins[6].wait()
    ins[7].wait()
    ins[8].wait()
    lamx[...] = expanded(lam)
    split_to(ext, fieldb[...], OWN)
    spread(ext)
    gamb[...] = joined(fieldb[...], lam, lamx)

    rowsc, rowse = wc.shape[0], base.shape[0]
    ins[4].wait()
    slots = rowse // 6
    lane = lax.broadcasted_iota(jnp.int32, (1, rowse), 1)
    owner = jnp.zeros((1, rowse), jnp.int32)
    for j in range(1, 6):
        owner = owner + jnp.where(lane >= slots * j, 1, 0)
    slot = lane - slots * owner
    repeat = lax.broadcasted_iota(jnp.int32, (slots - 1, rowse), 0) == slot - 1
    given = nn(colv[...].astype(F32).astype(BF16), repeat.astype(F32).astype(BF16))
    given = jnp.where(lax.broadcasted_iota(jnp.int32, given.shape, 0) == owner, given, 0.0)
    column = jnp.sum(given, axis=0, keepdims=True).astype(jnp.int32)
    column = jnp.where(slot == 0, owner, column)
    where = jnp.where(column < 9, column, jnp.where(column == 11, 9, column + 1))
    row = jnp.zeros((1, rowse), jnp.int32)
    for j in range(6):
        where = jnp.where(column == j, place[j], where)
        row = jnp.where(owner == j, place[j], row)
    target = row * 16 + (where & 1) * 8 + (where >> 1)
    pick = (
        lax.broadcasted_iota(jnp.int32, (rowsc, rowse), 0) == target
    ).astype(F32).astype(BF16)
    for i in range(4):
        base_copy(i).wait()
        for j in range(2):
            cols = slice(i * chunk + j * 512, i * chunk + j * 512 + 512)
            h, l = split2(base[:, cols])
            wc[:, cols] = nn(pick, h) + nn(pick, l)

    def lay(j, c):
        cols = pl.ds(pl.multiple_of(j * 128, 128), 128)
        for t in range(6):
            even = wc[t * 16 : t * 16 + 8, cols]
            odd = wc[t * 16 + 8 : t * 16 + 16, cols]
            wf[pl.ds(t * 64 + 2 * j, 8, stride=nodes + 1), :] = halves(even, swap(odd))
            wf[pl.ds(t * 64 + 2 * j + 1, 8, stride=nodes + 1), :] = halves(swap(even), odd)
        return c

    lax.fori_loop(0, 32, lay, 0, unroll=4)
    for q in (3, 4, 5, 0, 1, 2):
        h, l = split2(wf[q * (nodes + 1) : q * (nodes + 1) + nodes])
        whi[:, q * 128 : (q + 1) * 128] = h
        wlo[:, q * 128 : (q + 1) * 128] = l

    t_pair = (remote(ts.at[1], tr.at[0], 8, nxt), remote(ts.at[0], tr.at[1], 9, prev))

    def edges(src, cols, dot):
        left = src[0 : 2 * ROWS, cols] if dot is nt else src[0 : 2 * ROWS]
        both = dot(left, whi[:, cols])
        return both[0:ROWS] + both[ROWS : 2 * ROWS] + dot(left[0:ROWS], wlo[:, cols])

    def flux_pair(i):
        to_prev = remote(hs.at[i, 0], hr.at[i, 1], 2 * (2 + i) + 1, prev)
        to_next = remote(hs.at[i, 1], hr.at[i, 0], 2 * (2 + i), nxt)
        return to_next, to_prev

    def flux_and_weights(cols):
        fine = nn(xs[...], whi[:, cols])
        rest = jnp.concatenate([xs[0:ROWS], xs[2 * ROWS : 2 * ROWS + 16]], axis=0)
        rest = nn(rest, wlo[:, cols])
        return (
            fine[0:ROWS] + fine[ROWS : 2 * ROWS] + rest[0:ROWS],
            fine[2 * ROWS : 2 * ROWS + 16] + fine[2 * ROWS + 16 :] + rest[ROWS:],
        )

    def send_flux(i, flux):
        pack(hs.at[i, 0], hs.at[i, 1], flux[:, 0:128], flux[:, 128:256], flux[:, 256:384])
        send(*flux_pair(i))

    def outer(i):
        for t, tile in enumerate(unpack(fr.at[i, 0], fr.at[i, 1], HALF)):
            split_to(ext, tile, slice(384 + t * 128, 512 + t * 128))
        return edges(ext, AWAY, nt)

    def flux_in(i):
        arrive(*flux_pair(i))
        return jnp.concatenate(unpack(hr.at[i, 1], hr.at[i, 0], HALF), axis=1)

    def fold(x):
        total = x[0:8]
        for i in range(1, x.shape[0] // 8):
            total = total + x[8 * i : 8 * i + 8]
        return total

    def fold_wide(x):
        return fold(x[:, 0:128] + x[:, 128:256] + x[:, 256:384])

    def all_copy(i, off):
        return pltpu.make_async_remote_copy(
            src_ref=allb.at[i, me], dst_ref=allb.at[i, me],
            send_sem=all_send.at[i], recv_sem=all_recv.at[i],
            device_id={"space": lax.rem(me + off, n)}, device_id_type=MESH,
        )

    def send_products(i, x, rest, outside):
        weight = scale[1]
        packed = jnp.concatenate([weight, halves(weight[:HALF], weight[HALF:])], axis=0)
        weight = wide(weight)
        norm = jnp.sum(fold_wide(x * x * weight), axis=0, keepdims=True)
        product = fold_wide(x * rest * weight) - 2.0 * fold(outside * packed)
        product = jnp.sum(product, axis=0, keepdims=True)
        allb[i, me] = halves(norm + swap(norm), product + swap(product))

        def go(off, c):
            all_copy(i, off).start()
            return c

        lax.fori_loop(1, n, go, 0)

    def products(i):
        others = allb.at[i, pl.ds(0, n - 1)]
        pltpu.make_async_copy(others, others, all_recv.at[i]).wait()
        pltpu.make_async_copy(others, others, all_send.at[i]).wait()
        total = allb[i, 0]
        for d in range(1, n):
            total = total + allb[i, d]
        left = left_mask(1)
        return (
            jnp.sum(jnp.where(left, total, 0.0), keepdims=True),
            jnp.sum(jnp.where(left, 0.0, total), keepdims=True),
        )

    split_to(xs, gamb[...])
    h, l = split2(lam[...])
    xs[2 * ROWS : 2 * ROWS + 16] = h
    xs[2 * ROWS + 16 : 2 * ROWS + 32] = l
    flux, toward = flux_and_weights(AWAY)
    pack(ts.at[0], ts.at[1], toward[:, 0:128], toward[:, 128:256], toward[:, 256:384])
    send(*t_pair)
    send_flux(0, flux)
    flux, toward = flux_and_weights(OWN)
    backb[...] = -flux
    inner = edges(ext, OWN, nt)
    ones = jnp.ones((16, 768), BF16)
    row_total = (nt(ones, whi[...]) + nt(ones, wlo[...]))[0:1]
    arrive(*t_pair)
    came = jnp.concatenate(unpack(tr.at[1], tr.at[0], 8), axis=1)
    dmode[...] = toward + came + row_total * lam[...] + jnp.where(
        lax.broadcasted_iota(jnp.int32, (16, nodes), 0) == 8, cap, 0.0
    )
    dmodex[...] = expanded(dmode)
    cplb[...] = joined(fieldb[...], dmode, dmodex)
    arrive(*pair(fs.at[0], fr.at[0], 0))
    send_products(
        0, fieldb[...], cplb[...] + 2.0 * backb[...], hs[0, 0] * fr[0, 0] + hs[0, 1] * fr[0, 1]
    )
    z = inner + outer(0)
    split_to(xs, z)
    spread(xs)
    imageb[...] = cplb[...] + backb[...] - joined(z, lam, lamx)
    imageb[...] -= flux_in(0)
    send_field(1, imageb[...])

    split_to(ext, imageb[...], OWN)
    spread(ext)
    split_to(xs, joined(imageb[...], lam, lamx))
    send_flux(1, edges(xs, AWAY, nn))
    cplq[...] = joined(imageb[...], dmode, dmodex)
    backq[...] = -edges(xs, OWN, nn)
    inner = edges(ext, OWN, nt)
    norm0, product0 = products(0)
    step0 = norm0 / product0
    r1b[...] = fieldb[...] - step0 * imageb[...]
    cplb[...] = (cplb[...] + 2.0 * backb[...]) - step0 * (cplq[...] + 2.0 * backq[...])
    arrive(*pair(fs.at[1], fr.at[1], 1))
    outside = (hs[0, 0] - step0 * hs[1, 0]) * (fr[0, 0] - step0 * fr[1, 0])
    outside += (hs[0, 1] - step0 * hs[1, 1]) * (fr[0, 1] - step0 * fr[1, 1])
    send_products(1, r1b[...], cplb[...], outside)
    z = inner + outer(1)
    split_to(xs, z)
    spread(xs)
    cplq[...] = cplq[...] + backq[...] - joined(z, lam, lamx)

    def put_back(x):
        tiles = reorder([x[:, t * 128 : (t + 1) * 128] for t in range(3)], place)
        return jnp.concatenate([tile * scale[2] for tile in tiles], axis=1)

    def put_out(ref, y):
        for first, end, row in PLACES:
            ref[first:end] = y[row : row + end - first]

    fieldb[...] = put_back(r1b[...])
    norm1, product1 = products(1)
    ratio = norm1 / norm0
    step1 = norm1 / (product1 - ratio * norm1 / step0)
    put_out(x_ref, (step0 + step1 * ratio) * inp[0:ROWS] + step1 * fieldb[...])
    gamb[...] = fieldb[...] - (step1 * (1.0 + ratio) / step0) * (inp[0:ROWS] - fieldb[...])
    second = cplq[...] - flux_in(1)
    put_out(r_ref, gamb[...] + (step1 * step0) * put_back(second))

    for i in range(2):
        sent(*pair(fs.at[i], fr.at[i], i))
        sent(*flux_pair(i))
    sent(*t_pair)


def shards(right_side, capacity, base_cond, var_field, block_cols, send_list):
    n = lax.axis_size("space")
    terms, nodes = right_side.shape
    blocks, slots, area = base_cond.shape
    even, odd, expand, scales = chaos_tables()
    vmem = pl.BlockSpec(memory_space=pltpu.VMEM)
    field = pltpu.VMEM((ROWS, nodes), F32)
    small = pltpu.VMEM((16, nodes), F32)
    message = pltpu.VMEM((2, 2, MSG, 128), F32)
    return pl.pallas_call(
        functools.partial(kernel, n),
        out_shape=(
            pltpu.VMEM((terms, nodes), F32),
            pltpu.VMEM((terms, nodes), F32),
        ),
        in_specs=[pl.BlockSpec(memory_space=pltpu.HBM)] * 10,
        out_specs=(vmem, vmem),
        scratch_shapes=[
            pltpu.VMEM((terms, nodes), F32),
            pltpu.VMEM(var_field.shape, F32),
            pltpu.VMEM(capacity.shape, F32),
            pltpu.VMEM(block_cols.shape, jnp.int32),
            pltpu.SMEM(send_list.shape, jnp.int32),
            pltpu.VMEM(even.shape, BF16),
            pltpu.VMEM(odd.shape, BF16),
            pltpu.VMEM(expand.shape, BF16),
            pltpu.VMEM(scales.shape, F32),
            pltpu.VMEM((blocks * slots, area), F32),
            pltpu.VMEM((ROWS + 16, nodes), F32),
            pltpu.VMEM((blocks, ROWS + 16, 128), F32),
            pltpu.VMEM((blocks * 16, area), F32),
            pltpu.VMEM((8 * nodes + 8, 128), F32),
            pltpu.VMEM((nodes, 2 * nodes), BF16),
            pltpu.VMEM((nodes, 2 * nodes), BF16),
            pltpu.VMEM((VARS * EVEN + 432, nodes), F32),
            pltpu.VMEM((2 * ROWS + 32, nodes), BF16),
            pltpu.VMEM((2 * ROWS, 2 * nodes), BF16),
            small, pltpu.VMEM((384, nodes), F32), small, pltpu.VMEM((384, nodes), F32), small,
            field, field, field, field, field, field, field, field,
            message, message, message, message,
            pltpu.VMEM((2, 24, 128), F32),
            pltpu.VMEM((2, 24, 128), F32),
            pltpu.VMEM((2, n, 1, 128), F32),
            pltpu.SemaphoreType.DMA((9,)),
            pltpu.SemaphoreType.DMA((4,)),
            pltpu.SemaphoreType.DMA((10,)),
            pltpu.SemaphoreType.DMA((10,)),
            pltpu.SemaphoreType.DMA((2,)),
            pltpu.SemaphoreType.DMA((2,)),
        ],
        compiler_params=pltpu.CompilerParams(
            collective_id=0, has_side_effects=True, vmem_limit_bytes=60 * 1024 * 1024
        ),
        name="galerkin_cg",
    )(
        right_side, var_field, capacity, block_cols, send_list,
        jnp.asarray(even, BF16), jnp.asarray(odd, BF16), jnp.asarray(expand, BF16), jnp.asarray(scales),
        base_cond.reshape(blocks * slots, area),
    )


def solution(mesh):
    return jax.shard_map(
        shards,
        mesh=mesh,
        in_specs=(
            P(None, ("grp", "space")),
            P(("grp", "space")),
            P(("grp", "space"), None, None),
            P(None, ("grp", "space")),
            P(("grp", "space"), None),
            P(("grp", "space"), None, None),
        ),
        out_specs=(P(None, ("grp", "space")), P(None, ("grp", "space"))),
        check_vma=False,
    )
```

```python
import functools
import math

import jax
import jax.numpy as jnp
import numpy as np
from jax import lax
from jax.experimental import pallas as pl
from jax.experimental.pallas import tpu as pltpu
from jax.sharding import PartitionSpec as P

VARS = 8
ORDER = 3
ITERS = 2
SPREAD = 0.14
ROWS, EVEN, ODD, DEEP = 176, 40, 48, 56
PLACES = ((0, 1, 36), (1, 9, 48), (9, 45, 0), (45, 165, 56))
HALF = ROWS // 2
MSG = ROWS + HALF
OWN, AWAY = slice(0, 384), slice(384, 768)
MESH = pl.DeviceIdType.MESH
F32 = jnp.float32
BF16 = jnp.bfloat16


def chaos_tables():
    entries = []

    def grow(prefix, left):
        if len(prefix) == VARS:
            entries.append(tuple(prefix))
            return
        for degree in range(left + 1):
            grow(prefix + [degree], left - degree)

    grow([], ORDER)
    entries.sort(key=lambda m: (sum(m), tuple(-v for v in m)))
    lookup = {}
    for first, end, row in PLACES:
        for i in range(first, end):
            lookup[entries[i]] = row + i - first
    even = np.zeros((VARS * EVEN, 2 * (ROWS - ODD)), np.float32)
    odd = np.zeros((432, 2 * ODD), np.float32)
    expand = np.zeros((384, 16), np.float32)
    scale = np.ones((ROWS,), np.float64)
    for m, i in lookup.items():
        scale[i] = math.sqrt(math.prod(math.factorial(v) for v in m))
        held = [k for k in range(VARS) if m[k] > 0]
        for k in range(VARS):
            lowered = lookup.get(m[:k] + (m[k] - 1,) + m[k + 1 :])
            raised = lookup.get(m[:k] + (m[k] + 1,) + m[k + 1 :])
            for other, weight in ((lowered, m[k]), (raised, 1.0)):
                if other is None:
                    continue
                if i < EVEN:
                    even[EVEN * k + i, [other - ODD, ROWS - ODD + other - ODD]] = weight
                elif i < DEEP:
                    odd[8 * k + i - ODD, [other, ODD + other]] = weight
                else:
                    place = 120 * held.index(k) + i - DEEP
                    odd[64 + place, [other, ODD + other]] = weight
                    expand[place, k] = 1.0
    scales = np.stack([scale, 1.0 / scale**2], 0)
    scales = np.broadcast_to(scales[:, :, None], (2, ROWS, 128)).astype(np.float32)
    final = np.array([1.0 / scale[lookup[m]] for m in entries], np.float32)
    return even, odd, expand, scales, final


def split2(x):
    hi = x.astype(BF16)
    return hi, (x - hi.astype(F32)).astype(BF16)


def split3(x):
    hi = x.astype(BF16)
    rest = x - hi.astype(F32)
    mid = rest.astype(BF16)
    return hi, mid, (rest - mid.astype(F32)).astype(BF16)


def nn(a, b):
    return lax.dot_general(a, b, (((1,), (0,)), ((), ())), preferred_element_type=F32)


def nt(a, b):
    return lax.dot_general(a, b, (((1,), (1,)), ((), ())), preferred_element_type=F32)


def swap(x):
    return pltpu.roll(x, 64, 1)


def wide(x):
    return jnp.concatenate([x, x, x], axis=1)


def kernel(
    n,
    rhs_hbm, var_hbm, cap_hbm, cols_hbm, list_hbm, even_hbm, odd_hbm, expand_hbm, scale_hbm, base_hbm,
    x_ref, r_ref,
    rhs, var, capv, colv, lists, even, odd, expand, scale, base,
    inp, blk, wc, wf, whi, wlo, ybuf, xs, ext, lam, lamx, dmode, dmodex, caps,
    fieldb, gamb, cplb, backb, imageb, cplq, backq, r1b,
    fs, fr, hs, hr, ts, tr, allb,
    in_sem, base_sem, send_sem, recv_sem, all_send, all_recv,
):
    me = lax.axis_index("space")
    prev, nxt = lax.rem(me + n - 1, n), lax.rem(me + 1, n)
    chunk = base.shape[1] // 4

    ins = [
        pltpu.make_async_copy(src, dst, in_sem.at[i])
        for i, (src, dst) in enumerate(
            (
                (list_hbm, lists), (rhs_hbm, rhs), (var_hbm, var), (cap_hbm, capv),
                (cols_hbm, colv), (scale_hbm, scale), (even_hbm, even), (odd_hbm, odd),
                (expand_hbm, expand),
            )
        )
    ]

    def base_copy(i):
        cols = pl.ds(i * chunk, chunk)
        return pltpu.make_async_copy(base_hbm.at[:, cols], base.at[:, cols], base_sem.at[i])

    for copy in ins:
        copy.start()
    for i in range(4):
        base_copy(i).start()

    barrier = pltpu.get_barrier_semaphore()

    def greet(i, c):
        pl.semaphore_signal(
            barrier, inc=1, device_id={"space": lax.rem(me + i, n)}, device_id_type=MESH
        )
        return c

    lax.fori_loop(1, n, greet, 0)

    def remote(src, dst, which, peer):
        return pltpu.make_async_remote_copy(
            src_ref=src, dst_ref=dst, send_sem=send_sem.at[which], recv_sem=recv_sem.at[which],
            device_id={"space": peer}, device_id_type=MESH,
        )

    def pair(src, dst, e):
        return remote(src.at[0], dst.at[0], 2 * e, nxt), remote(src.at[1], dst.at[1], 2 * e + 1, prev)

    def send(up, down):
        @pl.when(me < n - 1)
        def _():
            up.start()

        @pl.when(me > 0)
        def _():
            down.start()

    def arrive(up, down):
        @pl.when(me > 0)
        def _():
            up.wait_recv()

        @pl.when(me < n - 1)
        def _():
            down.wait_recv()

    def sent(up, down):
        @pl.when(me < n - 1)
        def _():
            up.wait_send()

        @pl.when(me > 0)
        def _():
            down.wait_send()

    def left_mask(rows):
        return lax.broadcasted_iota(jnp.int32, (rows, 128), 1) < 64

    def halves(left_of, right_of):
        return jnp.where(left_mask(left_of.shape[0]), left_of, right_of)

    def pack(first_dst, last_dst, first, middle, last):
        half = middle.shape[0] // 2
        rows = first_dst.shape[0] - half
        top, low = middle[:half], middle[half:]
        first_dst[0:rows] = first[:rows]
        first_dst[rows : rows + half] = halves(top, swap(low))
        last_dst[0:rows] = last[:rows]
        last_dst[rows : rows + half] = halves(swap(top), low)

    def unpack(first_src, last_src, half):
        rows = first_src.shape[0] - half
        a, b = first_src[rows : rows + half], last_src[rows : rows + half]
        middle = jnp.concatenate([halves(a, swap(b)), halves(swap(a), b)], axis=0)
        first, last = first_src[0:rows], last_src[0:rows]
        if rows < 2 * half:
            pad = jnp.zeros((2 * half - rows, 128), F32)
            first = jnp.concatenate([first, pad], axis=0)
            last = jnp.concatenate([last, pad], axis=0)
        return first, middle, last

    @pl.when(me == 0)
    def _():
        for buf in (fr.at[0, 0], fr.at[1, 0], hr.at[0, 0], hr.at[1, 0], tr.at[0]):
            buf[...] = jnp.zeros(buf.shape, F32)

    @pl.when(me == n - 1)
    def _():
        for buf in (fr.at[0, 1], fr.at[1, 1], hr.at[0, 1], hr.at[1, 1], tr.at[1]):
            buf[...] = jnp.zeros(buf.shape, F32)

    nodes = rhs.shape[1]
    terms = rhs.shape[0]
    inp[...] = jnp.zeros_like(inp)
    for copy in ins[:4]:
        copy.wait()
    perm = [lists[0, 0, 0], lists[0, 0, 1], lists[0, 0, 2], lists[0, 1, 2], lists[0, 1, 0], lists[0, 1, 1]]
    place = []
    for r in range(6):
        at = jnp.int32(0)
        for t in range(1, 6):
            at = jnp.where(perm[t] == r, jnp.int32(t), at)
        place.append(at)
    for first, end, row in PLACES:
        inp[row : row + end - first] = rhs[first:end]
    inp[ROWS : ROWS + 8] = var[...]
    inp[ROWS + 8 : ROWS + 9] = capv[...].reshape(1, nodes)

    def reorder(tiles, index):
        rows = tiles[0].shape[0]
        for t in range(3):
            other = swap(tiles[t])
            blk[2 * t, 0:rows] = halves(tiles[t], other)
            blk[2 * t + 1, 0:rows] = halves(other, tiles[t])
        return [halves(blk[index[2 * t], 0:rows], blk[index[2 * t + 1], 0:rows]) for t in range(3)]

    moved = reorder([inp[:, t * 128 : (t + 1) * 128] for t in range(3)], perm)
    ins[5].wait()
    for t in range(3):
        cols = slice(t * 128, (t + 1) * 128)
        fieldb[:, cols] = moved[t][:ROWS] * scale[0]
        lam[0:8, cols] = moved[t][ROWS : ROWS + 8] * SPREAD
        caps[0:8, cols] = moved[t][ROWS + 8 : ROWS + 16]
    lam[8:9] = jnp.ones((1, nodes), F32)
    lam[9:16] = jnp.zeros((7, nodes), F32)
    cap = caps[0:1]

    pl.semaphore_wait(barrier, n - 1)

    def send_field(i, x):
        pack(fs.at[i, 0], fs.at[i, 1], x[:, 0:128], x[:, 128:256], x[:, 256:384])
        send(*pair(fs.at[i], fr.at[i], i))

    send_field(0, fieldb[...])

    def split_to(dst, x, cols=slice(None)):
        h, l = split2(x)
        dst[0:ROWS, cols] = h
        dst[ROWS : 2 * ROWS, cols] = l

    def spread(src):
        cols = OWN
        up = jnp.concatenate([src[ODD:ROWS, cols], src[ROWS + ODD : 2 * ROWS, cols]], axis=0)
        down = jnp.concatenate([src[0:ODD, cols], src[ROWS : ROWS + ODD, cols]], axis=0)
        ybuf[0 : VARS * EVEN] = nn(even[...], up)
        ybuf[VARS * EVEN :] = nn(odd[...], down)

    def joined(x, w, wx):
        top = w[8:9] * x[0:EVEN]
        one = w[8:9] * x[ODD:DEEP]
        low = w[8:9] * x[DEEP:ROWS]
        ones_at = VARS * EVEN
        for k in range(VARS):
            top = top + w[k : k + 1] * ybuf[EVEN * k : EVEN * (k + 1)]
            one = one + w[k : k + 1] * ybuf[ones_at + 8 * k : ones_at + 8 * (k + 1)]
        deep_at = ones_at + 64
        for s in range(3):
            low = low + wx[120 * s : 120 * s + 120] * ybuf[deep_at + 120 * s : deep_at + 120 * s + 120]
        return jnp.concatenate([top, jnp.zeros((ODD - EVEN, nodes), F32), one, low], axis=0)

    def expanded(w):
        h, m, l = split3(w[...])
        e = expand[...]
        return nn(e, h) + (nn(e, m) + nn(e, l))

    ins[6].wait()
    ins[7].wait()
    ins[8].wait()
    lamx[...] = expanded(lam)
    split_to(ext, fieldb[...], OWN)
    spread(ext)
    gamb[...] = joined(fieldb[...], lam, lamx)

    rowsc, rowse = wc.shape[0], base.shape[0]
    ins[4].wait()
    slots = rowse // 6
    lane = lax.broadcasted_iota(jnp.int32, (1, rowse), 1)
    owner = jnp.zeros((1, rowse), jnp.int32)
    for j in range(1, 6):
        owner = owner + jnp.where(lane >= slots * j, 1, 0)
    slot = lane - slots * owner
    repeat = lax.broadcasted_iota(jnp.int32, (slots - 1, rowse), 0) == slot - 1
    given = nn(colv[...].astype(F32).astype(BF16), repeat.astype(F32).astype(BF16))
    given = jnp.where(lax.broadcasted_iota(jnp.int32, given.shape, 0) == owner, given, 0.0)
    column = jnp.sum(given, axis=0, keepdims=True).astype(jnp.int32)
    column = jnp.where(slot == 0, owner, column)
    where = jnp.where(column < 9, column, jnp.where(column == 11, 9, column + 1))
    row = jnp.zeros((1, rowse), jnp.int32)
    for j in range(6):
        where = jnp.where(column == j, place[j], where)
        row = jnp.where(owner == j, place[j], row)
    target = row * 16 + (where & 1) * 8 + (where >> 1)
    pick = (
        lax.broadcasted_iota(jnp.int32, (rowsc, rowse), 0) == target
    ).astype(F32).astype(BF16)
    for i in range(4):
        base_copy(i).wait()
        for j in range(2):
            cols = slice(i * chunk + j * 512, i * chunk + j * 512 + 512)
            h, l = split2(base[:, cols])
            wc[:, cols] = nn(pick, h) + nn(pick, l)

    def lay(j, c):
        cols = pl.ds(pl.multiple_of(j * 128, 128), 128)
        for t in range(6):
            even = wc[t * 16 : t * 16 + 8, cols]
            odd = wc[t * 16 + 8 : t * 16 + 16, cols]
            wf[pl.ds(t * 64 + 2 * j, 8, stride=nodes + 1), :] = halves(even, swap(odd))
            wf[pl.ds(t * 64 + 2 * j + 1, 8, stride=nodes + 1), :] = halves(swap(even), odd)
        return c

    lax.fori_loop(0, 32, lay, 0, unroll=4)
    for q in (3, 4, 5, 0, 1, 2):
        h, l = split2(wf[q * (nodes + 1) : q * (nodes + 1) + nodes])
        whi[:, q * 128 : (q + 1) * 128] = h
        wlo[:, q * 128 : (q + 1) * 128] = l

    t_pair = (remote(ts.at[1], tr.at[0], 8, nxt), remote(ts.at[0], tr.at[1], 9, prev))

    def edges(src, cols, dot):
        left = src[0 : 2 * ROWS, cols] if dot is nt else src[0 : 2 * ROWS]
        both = dot(left, whi[:, cols])
        return both[0:ROWS] + both[ROWS : 2 * ROWS] + dot(left[0:ROWS], wlo[:, cols])

    def flux_pair(i):
        to_prev = remote(hs.at[i, 0], hr.at[i, 1], 2 * (2 + i) + 1, prev)
        to_next = remote(hs.at[i, 1], hr.at[i, 0], 2 * (2 + i), nxt)
        return to_next, to_prev

    def flux_and_weights(cols):
        fine = nn(xs[...], whi[:, cols])
        rest = jnp.concatenate([xs[0:ROWS], xs[2 * ROWS : 2 * ROWS + 16]], axis=0)
        rest = nn(rest, wlo[:, cols])
        return (
            fine[0:ROWS] + fine[ROWS : 2 * ROWS] + rest[0:ROWS],
            fine[2 * ROWS : 2 * ROWS + 16] + fine[2 * ROWS + 16 :] + rest[ROWS:],
        )

    def send_flux(i, flux):
        pack(hs.at[i, 0], hs.at[i, 1], flux[:, 0:128], flux[:, 128:256], flux[:, 256:384])
        send(*flux_pair(i))

    def outer(i):
        for t, tile in enumerate(unpack(fr.at[i, 0], fr.at[i, 1], HALF)):
            split_to(ext, tile, slice(384 + t * 128, 512 + t * 128))
        return edges(ext, AWAY, nt)

    def flux_in(i):
        arrive(*flux_pair(i))
        return jnp.concatenate(unpack(hr.at[i, 1], hr.at[i, 0], HALF), axis=1)

    def fold(x):
        total = x[0:8]
        for i in range(1, x.shape[0] // 8):
            total = total + x[8 * i : 8 * i + 8]
        return total

    def fold_wide(x):
        return fold(x[:, 0:128] + x[:, 128:256] + x[:, 256:384])

    def all_copy(i, off):
        return pltpu.make_async_remote_copy(
            src_ref=allb.at[i, me], dst_ref=allb.at[i, me],
            send_sem=all_send.at[i], recv_sem=all_recv.at[i],
            device_id={"space": lax.rem(me + off, n)}, device_id_type=MESH,
        )

    def send_products(i, x, rest, outside):
        weight = scale[1]
        packed = jnp.concatenate([weight, halves(weight[:HALF], weight[HALF:])], axis=0)
        weight = wide(weight)
        norm = jnp.sum(fold_wide(x * x * weight), axis=0, keepdims=True)
        product = fold_wide(x * rest * weight) - 2.0 * fold(outside * packed)
        product = jnp.sum(product, axis=0, keepdims=True)
        allb[i, me] = halves(norm + swap(norm), product + swap(product))

        def go(off, c):
            all_copy(i, off).start()
            return c

        lax.fori_loop(1, n, go, 0)

    def products(i):
        others = allb.at[i, pl.ds(0, n - 1)]
        pltpu.make_async_copy(others, others, all_recv.at[i]).wait()
        pltpu.make_async_copy(others, others, all_send.at[i]).wait()
        total = allb[i, 0]
        for d in range(1, n):
            total = total + allb[i, d]
        left = left_mask(1)
        return (
            jnp.sum(jnp.where(left, total, 0.0), keepdims=True),
            jnp.sum(jnp.where(left, 0.0, total), keepdims=True),
        )

    split_to(xs, gamb[...])
    h, l = split2(lam[...])
    xs[2 * ROWS : 2 * ROWS + 16] = h
    xs[2 * ROWS + 16 : 2 * ROWS + 32] = l
    flux, toward = flux_and_weights(AWAY)
    pack(ts.at[0], ts.at[1], toward[:, 0:128], toward[:, 128:256], toward[:, 256:384])
    send(*t_pair)
    send_flux(0, flux)
    flux, toward = flux_and_weights(OWN)
    backb[...] = -flux
    inner = edges(ext, OWN, nt)
    ones = jnp.ones((16, 768), BF16)
    row_total = (nt(ones, whi[...]) + nt(ones, wlo[...]))[0:1]
    arrive(*t_pair)
    came = jnp.concatenate(unpack(tr.at[1], tr.at[0], 8), axis=1)
    dmode[...] = toward + came + row_total * lam[...] + jnp.where(
        lax.broadcasted_iota(jnp.int32, (16, nodes), 0) == 8, cap, 0.0
    )
    dmodex[...] = expanded(dmode)
    cplb[...] = joined(fieldb[...], dmode, dmodex)
    arrive(*pair(fs.at[0], fr.at[0], 0))
    send_products(
        0, fieldb[...], cplb[...] + 2.0 * backb[...], hs[0, 0] * fr[0, 0] + hs[0, 1] * fr[0, 1]
    )
    z = inner + outer(0)
    split_to(xs, z)
    spread(xs)
    imageb[...] = cplb[...] + backb[...] - joined(z, lam, lamx)
    send_field(1, imageb[...])
    imageb[...] -= flux_in(0)

    split_to(ext, imageb[...], OWN)
    spread(ext)
    split_to(xs, joined(imageb[...], lam, lamx))
    send_flux(1, edges(xs, AWAY, nn))
    cplq[...] = joined(imageb[...], dmode, dmodex)
    backq[...] = -edges(xs, OWN, nn)
    inner = edges(ext, OWN, nt)
    norm0, product0 = products(0)
    step0 = norm0 / product0
    r1b[...] = fieldb[...] - step0 * imageb[...]
    cplb[...] = (cplb[...] + 2.0 * backb[...]) - step0 * (cplq[...] + 2.0 * backq[...])
    arrive(*pair(fs.at[1], fr.at[1], 1))
    fr[1] = fr[1] - hs[0]
    outside = (hs[0, 0] - step0 * hs[1, 0]) * (fr[0, 0] - step0 * fr[1, 0])
    outside += (hs[0, 1] - step0 * hs[1, 1]) * (fr[0, 1] - step0 * fr[1, 1])
    send_products(1, r1b[...], cplb[...], outside)
    z = inner + outer(1)
    split_to(xs, z)
    spread(xs)
    cplq[...] = cplq[...] + backq[...] - joined(z, lam, lamx)

    def put_back(x):
        tiles = reorder([x[:, t * 128 : (t + 1) * 128] for t in range(3)], place)
        return jnp.concatenate(tiles, axis=1)

    def put_out(ref, y):
        for first, end, row in PLACES:
            ref[first:end] = y[row : row + end - first]

    inp[0:ROWS] = inp[0:ROWS] * wide(scale[0])
    fieldb[...] = put_back(r1b[...])
    norm1, product1 = products(1)
    ratio = norm1 / norm0
    step1 = norm1 / (product1 - ratio * norm1 / step0)
    put_out(x_ref, (step0 + step1 * ratio) * inp[0:ROWS] + step1 * fieldb[...])
    gamb[...] = fieldb[...] - (step1 * (1.0 + ratio) / step0) * (inp[0:ROWS] - fieldb[...])
    second = cplq[...] - flux_in(1)
    put_out(r_ref, gamb[...] + (step1 * step0) * put_back(second))

    for i in range(2):
        sent(*pair(fs.at[i], fr.at[i], i))
        sent(*flux_pair(i))
    sent(*t_pair)


def shards(right_side, capacity, base_cond, var_field, block_cols, send_list):
    n = lax.axis_size("space")
    terms, nodes = right_side.shape
    blocks, slots, area = base_cond.shape
    even, odd, expand, scales, final = chaos_tables()
    vmem = pl.BlockSpec(memory_space=pltpu.VMEM)
    field = pltpu.VMEM((ROWS, nodes), F32)
    small = pltpu.VMEM((16, nodes), F32)
    message = pltpu.VMEM((2, 2, MSG, 128), F32)
    scaled = pl.pallas_call(
        functools.partial(kernel, n),
        out_shape=(
            pltpu.VMEM((terms, nodes), F32),
            pltpu.VMEM((terms, nodes), F32),
        ),
        in_specs=[pl.BlockSpec(memory_space=pltpu.HBM)] * 10,
        out_specs=(vmem, vmem),
        scratch_shapes=[
            pltpu.VMEM((terms, nodes), F32),
            pltpu.VMEM(var_field.shape, F32),
            pltpu.VMEM(capacity.shape, F32),
            pltpu.VMEM(block_cols.shape, jnp.int32),
            pltpu.SMEM(send_list.shape, jnp.int32),
            pltpu.VMEM(even.shape, BF16),
            pltpu.VMEM(odd.shape, BF16),
            pltpu.VMEM(expand.shape, BF16),
            pltpu.VMEM(scales.shape, F32),
            pltpu.VMEM((blocks * slots, area), F32),
            pltpu.VMEM((ROWS + 16, nodes), F32),
            pltpu.VMEM((blocks, ROWS + 16, 128), F32),
            pltpu.VMEM((blocks * 16, area), F32),
            pltpu.VMEM((8 * nodes + 8, 128), F32),
            pltpu.VMEM((nodes, 2 * nodes), BF16),
            pltpu.VMEM((nodes, 2 * nodes), BF16),
            pltpu.VMEM((VARS * EVEN + 432, nodes), F32),
            pltpu.VMEM((2 * ROWS + 32, nodes), BF16),
            pltpu.VMEM((2 * ROWS, 2 * nodes), BF16),
            small, pltpu.VMEM((384, nodes), F32), small, pltpu.VMEM((384, nodes), F32), small,
            field, field, field, field, field, field, field, field,
            message, message, message, message,
            pltpu.VMEM((2, 24, 128), F32),
            pltpu.VMEM((2, 24, 128), F32),
            pltpu.VMEM((2, n, 1, 128), F32),
            pltpu.SemaphoreType.DMA((9,)),
            pltpu.SemaphoreType.DMA((4,)),
            pltpu.SemaphoreType.DMA((10,)),
            pltpu.SemaphoreType.DMA((10,)),
            pltpu.SemaphoreType.DMA((2,)),
            pltpu.SemaphoreType.DMA((2,)),
        ],
        compiler_params=pltpu.CompilerParams(
            collective_id=0, has_side_effects=True, vmem_limit_bytes=60 * 1024 * 1024
        ),
        name="galerkin_cg",
    )(
        right_side, var_field, capacity, block_cols, send_list,
        jnp.asarray(even, BF16), jnp.asarray(odd, BF16), jnp.asarray(expand, BF16), jnp.asarray(scales),
        base_cond.reshape(blocks * slots, area),
    )
    final = jnp.asarray(final)[:, None]
    return scaled[0] * final, scaled[1] * final


def solution(mesh):
    return jax.shard_map(
        shards,
        mesh=mesh,
        in_specs=(
            P(None, ("grp", "space")),
            P(("grp", "space")),
            P(("grp", "space"), None, None),
            P(None, ("grp", "space")),
            P(("grp", "space"), None),
            P(("grp", "space"), None, None),
        ),
        out_specs=(P(None, ("grp", "space")), P(None, ("grp", "space"))),
        check_vma=False,
    )
```

```python
import functools
import math

import jax
import jax.numpy as jnp
import numpy as np
from jax import lax
from jax.experimental import pallas as pl
from jax.experimental.pallas import tpu as pltpu
from jax.sharding import PartitionSpec as P

VARS = 8
ORDER = 3
ITERS = 2
SPREAD = 0.14
ROWS, EVEN, ODD, DEEP = 176, 40, 48, 56
PLACES = ((0, 1, 36), (1, 9, 48), (9, 45, 0), (45, 165, 56))
HALF = ROWS // 2
MSG = ROWS + HALF
OWN, AWAY = slice(0, 384), slice(384, 768)
MESH = pl.DeviceIdType.MESH
F32 = jnp.float32
BF16 = jnp.bfloat16


def chaos_tables():
    entries = []

    def grow(prefix, left):
        if len(prefix) == VARS:
            entries.append(tuple(prefix))
            return
        for degree in range(left + 1):
            grow(prefix + [degree], left - degree)

    grow([], ORDER)
    entries.sort(key=lambda m: (sum(m), tuple(-v for v in m)))
    lookup = {}
    for first, end, row in PLACES:
        for i in range(first, end):
            lookup[entries[i]] = row + i - first
    even = np.zeros((VARS * EVEN, 2 * (ROWS - ODD)), np.float32)
    odd = np.zeros((432, 2 * ODD), np.float32)
    expand = np.zeros((384, 16), np.float32)
    scale = np.ones((ROWS,), np.float64)
    for m, i in lookup.items():
        scale[i] = math.sqrt(math.prod(math.factorial(v) for v in m))
        held = [k for k in range(VARS) if m[k] > 0]
        for k in range(VARS):
            lowered = lookup.get(m[:k] + (m[k] - 1,) + m[k + 1 :])
            raised = lookup.get(m[:k] + (m[k] + 1,) + m[k + 1 :])
            for other, weight in ((lowered, m[k]), (raised, 1.0)):
                if other is None:
                    continue
                if i < EVEN:
                    even[EVEN * k + i, [other - ODD, ROWS - ODD + other - ODD]] = weight
                elif i < DEEP:
                    odd[8 * k + i - ODD, [other, ODD + other]] = weight
                else:
                    place = 120 * held.index(k) + i - DEEP
                    odd[64 + place, [other, ODD + other]] = weight
                    expand[place, k] = 1.0
    scales = np.stack([scale, 1.0 / scale**2], 0)
    scales = np.broadcast_to(scales[:, :, None], (2, ROWS, 128)).astype(np.float32)
    final = np.array([1.0 / scale[lookup[m]] for m in entries], np.float32)
    return even, odd, expand, scales, final


def split2(x):
    hi = x.astype(BF16)
    return hi, (x - hi.astype(F32)).astype(BF16)


def split3(x):
    hi = x.astype(BF16)
    rest = x - hi.astype(F32)
    mid = rest.astype(BF16)
    return hi, mid, (rest - mid.astype(F32)).astype(BF16)


def nn(a, b):
    return lax.dot_general(a, b, (((1,), (0,)), ((), ())), preferred_element_type=F32)


def nt(a, b):
    return lax.dot_general(a, b, (((1,), (1,)), ((), ())), preferred_element_type=F32)


def swap(x):
    return pltpu.roll(x, 64, 1)


def wide(x):
    return jnp.concatenate([x, x, x], axis=1)


def kernel(
    n,
    rhs_hbm, var_hbm, cap_hbm, cols_hbm, list_hbm, even_hbm, odd_hbm, expand_hbm, scale_hbm, base_hbm,
    x_ref, r_ref,
    rhs, var, capv, colv, lists, even, odd, expand, scale, base,
    inp, blk, wc, wf, whi, wlo, ybuf, xs, ext, lam, lamx, dmode, dmodex, caps,
    fieldb, gamb, cplb, backb, imageb, cplq, backq, r1b,
    fs, fr, hs, hr, ts, tr, allb,
    in_sem, base_sem, send_sem, recv_sem, all_send, all_recv,
):
    me = lax.axis_index("space")
    prev, nxt = lax.rem(me + n - 1, n), lax.rem(me + 1, n)
    chunk = base.shape[1] // 4

    ins = [
        pltpu.make_async_copy(src, dst, in_sem.at[i])
        for i, (src, dst) in enumerate(
            (
                (list_hbm, lists), (rhs_hbm, rhs), (var_hbm, var), (cap_hbm, capv),
                (cols_hbm, colv), (scale_hbm, scale), (even_hbm, even), (odd_hbm, odd),
                (expand_hbm, expand),
            )
        )
    ]

    def base_copy(i):
        cols = pl.ds(i * chunk, chunk)
        return pltpu.make_async_copy(base_hbm.at[:, cols], base.at[:, cols], base_sem.at[i])

    for copy in ins:
        copy.start()
    for i in range(4):
        base_copy(i).start()

    barrier = pltpu.get_barrier_semaphore()

    def greet(i, c):
        pl.semaphore_signal(
            barrier, inc=1, device_id={"space": lax.rem(me + i, n)}, device_id_type=MESH
        )
        return c

    lax.fori_loop(1, n, greet, 0)

    def remote(src, dst, which, peer):
        return pltpu.make_async_remote_copy(
            src_ref=src, dst_ref=dst, send_sem=send_sem.at[which], recv_sem=recv_sem.at[which],
            device_id={"space": peer}, device_id_type=MESH,
        )

    def pair(src, dst, e):
        return remote(src.at[0], dst.at[0], 2 * e, nxt), remote(src.at[1], dst.at[1], 2 * e + 1, prev)

    def send(up, down):
        @pl.when(me < n - 1)
        def _():
            up.start()

        @pl.when(me > 0)
        def _():
            down.start()

    def arrive(up, down):
        @pl.when(me > 0)
        def _():
            up.wait_recv()

        @pl.when(me < n - 1)
        def _():
            down.wait_recv()

    def sent(up, down):
        @pl.when(me < n - 1)
        def _():
            up.wait_send()

        @pl.when(me > 0)
        def _():
            down.wait_send()

    def left_mask(rows):
        return lax.broadcasted_iota(jnp.int32, (rows, 128), 1) < 64

    def halves(left_of, right_of):
        return jnp.where(left_mask(left_of.shape[0]), left_of, right_of)

    def pack(first_dst, last_dst, first, middle, last):
        half = middle.shape[0] // 2
        rows = first_dst.shape[0] - half
        top, low = middle[:half], middle[half:]
        first_dst[0:rows] = first[:rows]
        first_dst[rows : rows + half] = halves(top, swap(low))
        last_dst[0:rows] = last[:rows]
        last_dst[rows : rows + half] = halves(swap(top), low)

    def unpack(first_src, last_src, half):
        rows = first_src.shape[0] - half
        a, b = first_src[rows : rows + half], last_src[rows : rows + half]
        middle = jnp.concatenate([halves(a, swap(b)), halves(swap(a), b)], axis=0)
        first, last = first_src[0:rows], last_src[0:rows]
        if rows < 2 * half:
            pad = jnp.zeros((2 * half - rows, 128), F32)
            first = jnp.concatenate([first, pad], axis=0)
            last = jnp.concatenate([last, pad], axis=0)
        return first, middle, last

    @pl.when(me == 0)
    def _():
        for buf in (fr.at[0, 0], fr.at[1, 0], hr.at[0, 0], hr.at[1, 0], tr.at[0]):
            buf[...] = jnp.zeros(buf.shape, F32)

    @pl.when(me == n - 1)
    def _():
        for buf in (fr.at[0, 1], fr.at[1, 1], hr.at[0, 1], hr.at[1, 1], tr.at[1]):
            buf[...] = jnp.zeros(buf.shape, F32)

    nodes = rhs.shape[1]
    terms = rhs.shape[0]
    inp[...] = jnp.zeros_like(inp)
    for copy in ins[:4]:
        copy.wait()
    perm = [lists[0, 0, 0], lists[0, 0, 1], lists[0, 0, 2], lists[0, 1, 2], lists[0, 1, 0], lists[0, 1, 1]]
    place = []
    for r in range(6):
        at = jnp.int32(0)
        for t in range(1, 6):
            at = jnp.where(perm[t] == r, jnp.int32(t), at)
        place.append(at)
    for first, end, row in PLACES:
        inp[row : row + end - first] = rhs[first:end]
    inp[ROWS : ROWS + 8] = var[...]
    inp[ROWS + 8 : ROWS + 9] = capv[...].reshape(1, nodes)

    def reorder(tiles, index):
        rows = tiles[0].shape[0]
        for t in range(3):
            other = swap(tiles[t])
            blk[2 * t, 0:rows] = halves(tiles[t], other)
            blk[2 * t + 1, 0:rows] = halves(other, tiles[t])
        return [halves(blk[index[2 * t], 0:rows], blk[index[2 * t + 1], 0:rows]) for t in range(3)]

    moved = reorder([inp[:, t * 128 : (t + 1) * 128] for t in range(3)], perm)
    ins[5].wait()
    for t in range(3):
        cols = slice(t * 128, (t + 1) * 128)
        fieldb[:, cols] = moved[t][:ROWS] * scale[0]
        lam[0:8, cols] = moved[t][ROWS : ROWS + 8] * SPREAD
        caps[0:8, cols] = moved[t][ROWS + 8 : ROWS + 16]
    lam[8:9] = jnp.ones((1, nodes), F32)
    lam[9:16] = jnp.zeros((7, nodes), F32)
    cap = caps[0:1]

    pl.semaphore_wait(barrier, n - 1)

    def send_field(i, x):
        pack(fs.at[i, 0], fs.at[i, 1], x[:, 0:128], x[:, 128:256], x[:, 256:384])
        send(*pair(fs.at[i], fr.at[i], i))

    send_field(0, fieldb[...])

    def split_to(dst, x, cols=slice(None)):
        h, l = split2(x)
        dst[0:ROWS, cols] = h
        dst[ROWS : 2 * ROWS, cols] = l

    def spread(src):
        cols = OWN
        up = jnp.concatenate([src[ODD:ROWS, cols], src[ROWS + ODD : 2 * ROWS, cols]], axis=0)
        down = jnp.concatenate([src[0:ODD, cols], src[ROWS : ROWS + ODD, cols]], axis=0)
        ybuf[0 : VARS * EVEN] = nn(even[...], up)
        ybuf[VARS * EVEN :] = nn(odd[...], down)

    def joined(x, w, wx):
        top = w[8:9] * x[0:EVEN]
        one = w[8:9] * x[ODD:DEEP]
        low = w[8:9] * x[DEEP:ROWS]
        ones_at = VARS * EVEN
        for k in range(VARS):
            top = top + w[k : k + 1] * ybuf[EVEN * k : EVEN * (k + 1)]
            one = one + w[k : k + 1] * ybuf[ones_at + 8 * k : ones_at + 8 * (k + 1)]
        deep_at = ones_at + 64
        for s in range(3):
            low = low + wx[120 * s : 120 * s + 120] * ybuf[deep_at + 120 * s : deep_at + 120 * s + 120]
        return jnp.concatenate([top, jnp.zeros((ODD - EVEN, nodes), F32), one, low], axis=0)

    def expanded(w):
        h, m, l = split3(w[...])
        e = expand[...]
        return nn(e, h) + (nn(e, m) + nn(e, l))

    ins[6].wait()
    ins[7].wait()
    ins[8].wait()
    lamx[...] = expanded(lam)
    split_to(ext, fieldb[...], OWN)
    spread(ext)
    gamb[...] = joined(fieldb[...], lam, lamx)

    rowsc, rowse = wc.shape[0], base.shape[0]
    ins[4].wait()
    slots = rowse // 6
    lane = lax.broadcasted_iota(jnp.int32, (1, rowse), 1)
    owner = jnp.zeros((1, rowse), jnp.int32)
    for j in range(1, 6):
        owner = owner + jnp.where(lane >= slots * j, 1, 0)
    slot = lane - slots * owner
    repeat = lax.broadcasted_iota(jnp.int32, (slots - 1, rowse), 0) == slot - 1
    given = nn(colv[...].astype(F32).astype(BF16), repeat.astype(F32).astype(BF16))
    given = jnp.where(lax.broadcasted_iota(jnp.int32, given.shape, 0) == owner, given, 0.0)
    column = jnp.sum(given, axis=0, keepdims=True).astype(jnp.int32)
    column = jnp.where(slot == 0, owner, column)
    where = jnp.where(column < 9, column, jnp.where(column == 11, 9, column + 1))
    row = jnp.zeros((1, rowse), jnp.int32)
    for j in range(6):
        where = jnp.where(column == j, place[j], where)
        row = jnp.where(owner == j, place[j], row)
    target = row * 16 + (where & 1) * 8 + (where >> 1)
    pick = (
        lax.broadcasted_iota(jnp.int32, (rowsc, rowse), 0) == target
    ).astype(F32).astype(BF16)
    for i in range(4):
        base_copy(i).wait()

    def merge(j, c):
        cols = pl.ds(pl.multiple_of(j * 512, 512), 512)
        h, l = split2(base[:, cols])
        wc[:, cols] = nn(pick, h) + nn(pick, l)
        return c

    lax.fori_loop(0, base.shape[1] // 512, merge, 0)

    def lay(j, c):
        cols = pl.ds(pl.multiple_of(j * 128, 128), 128)
        for t in range(6):
            even = wc[t * 16 : t * 16 + 8, cols]
            odd = wc[t * 16 + 8 : t * 16 + 16, cols]
            wf[pl.ds(t * 64 + 2 * j, 8, stride=nodes + 1), :] = halves(even, swap(odd))
            wf[pl.ds(t * 64 + 2 * j + 1, 8, stride=nodes + 1), :] = halves(swap(even), odd)
        return c

    lax.fori_loop(0, 32, lay, 0, unroll=4)

    def halve(q, c):
        cols = pl.ds(pl.multiple_of(q * 128, 128), 128)
        h, l = split2(wf[pl.ds(q * (nodes + 1), nodes)])
        whi[:, cols] = h
        wlo[:, cols] = l
        return c

    lax.fori_loop(0, 6, halve, 0)

    t_pair = (remote(ts.at[1], tr.at[0], 8, nxt), remote(ts.at[0], tr.at[1], 9, prev))

    def edges(src, cols, dot):
        left = src[0 : 2 * ROWS, cols] if dot is nt else src[0 : 2 * ROWS]
        both = dot(left, whi[:, cols])
        return both[0:ROWS] + both[ROWS : 2 * ROWS] + dot(left[0:ROWS], wlo[:, cols])

    def flux_pair(i):
        to_prev = remote(hs.at[i, 0], hr.at[i, 1], 2 * (2 + i) + 1, prev)
        to_next = remote(hs.at[i, 1], hr.at[i, 0], 2 * (2 + i), nxt)
        return to_next, to_prev

    def flux_and_weights(cols):
        fine = nn(xs[...], whi[:, cols])
        rest = jnp.concatenate([xs[0:ROWS], xs[2 * ROWS : 2 * ROWS + 16]], axis=0)
        rest = nn(rest, wlo[:, cols])
        return (
            fine[0:ROWS] + fine[ROWS : 2 * ROWS] + rest[0:ROWS],
            fine[2 * ROWS : 2 * ROWS + 16] + fine[2 * ROWS + 16 :] + rest[ROWS:],
        )

    def send_flux(i, flux):
        pack(hs.at[i, 0], hs.at[i, 1], flux[:, 0:128], flux[:, 128:256], flux[:, 256:384])
        send(*flux_pair(i))

    def outer(i):
        for t, tile in enumerate(unpack(fr.at[i, 0], fr.at[i, 1], HALF)):
            split_to(ext, tile, slice(384 + t * 128, 512 + t * 128))
        return edges(ext, AWAY, nt)

    def flux_in(i):
        arrive(*flux_pair(i))
        return jnp.concatenate(unpack(hr.at[i, 1], hr.at[i, 0], HALF), axis=1)

    def fold(x):
        total = x[0:8]
        for i in range(1, x.shape[0] // 8):
            total = total + x[8 * i : 8 * i + 8]
        return total

    def fold_wide(x):
        return fold(x[:, 0:128] + x[:, 128:256] + x[:, 256:384])

    def all_copy(i, off):
        return pltpu.make_async_remote_copy(
            src_ref=allb.at[i, me], dst_ref=allb.at[i, me],
            send_sem=all_send.at[i], recv_sem=all_recv.at[i],
            device_id={"space": lax.rem(me + off, n)}, device_id_type=MESH,
        )

    def send_products(i, x, rest, outside):
        weight = scale[1]
        packed = jnp.concatenate([weight, halves(weight[:HALF], weight[HALF:])], axis=0)
        weight = wide(weight)
        norm = jnp.sum(fold_wide(x * x * weight), axis=0, keepdims=True)
        product = fold_wide(x * rest * weight) - 2.0 * fold(outside * packed)
        product = jnp.sum(product, axis=0, keepdims=True)
        allb[i, me] = halves(norm + swap(norm), product + swap(product))

        def go(off, c):
            all_copy(i, off).start()
            return c

        lax.fori_loop(1, n, go, 0)

    def products(i):
        others = allb.at[i, pl.ds(0, n - 1)]
        pltpu.make_async_copy(others, others, all_recv.at[i]).wait()
        pltpu.make_async_copy(others, others, all_send.at[i]).wait()
        total = allb[i, 0]
        for d in range(1, n):
            total = total + allb[i, d]
        left = left_mask(1)
        return (
            jnp.sum(jnp.where(left, total, 0.0), keepdims=True),
            jnp.sum(jnp.where(left, 0.0, total), keepdims=True),
        )

    split_to(xs, gamb[...])
    h, l = split2(lam[...])
    xs[2 * ROWS : 2 * ROWS + 16] = h
    xs[2 * ROWS + 16 : 2 * ROWS + 32] = l
    flux, toward = flux_and_weights(AWAY)
    pack(ts.at[0], ts.at[1], toward[:, 0:128], toward[:, 128:256], toward[:, 256:384])
    send(*t_pair)
    send_flux(0, flux)
    flux, toward = flux_and_weights(OWN)
    backb[...] = -flux
    inner = edges(ext, OWN, nt)
    ones = jnp.ones((16, 768), BF16)
    row_total = (nt(ones, whi[...]) + nt(ones, wlo[...]))[0:1]
    arrive(*t_pair)
    came = jnp.concatenate(unpack(tr.at[1], tr.at[0], 8), axis=1)
    dmode[...] = toward + came + row_total * lam[...] + jnp.where(
        lax.broadcasted_iota(jnp.int32, (16, nodes), 0) == 8, cap, 0.0
    )
    dmodex[...] = expanded(dmode)
    cplb[...] = joined(fieldb[...], dmode, dmodex)
    arrive(*pair(fs.at[0], fr.at[0], 0))
    send_products(
        0, fieldb[...], cplb[...] + 2.0 * backb[...], hs[0, 0] * fr[0, 0] + hs[0, 1] * fr[0, 1]
    )
    z = inner + outer(0)
    split_to(xs, z)
    spread(xs)
    imageb[...] = cplb[...] + backb[...] - joined(z, lam, lamx)
    send_field(1, imageb[...])
    imageb[...] -= flux_in(0)

    split_to(ext, imageb[...], OWN)
    spread(ext)
    split_to(xs, joined(imageb[...], lam, lamx))
    send_flux(1, edges(xs, AWAY, nn))
    cplq[...] = joined(imageb[...], dmode, dmodex)
    backq[...] = -edges(xs, OWN, nn)
    inner = edges(ext, OWN, nt)
    norm0, product0 = products(0)
    step0 = norm0 / product0
    r1b[...] = fieldb[...] - step0 * imageb[...]
    cplb[...] = (cplb[...] + 2.0 * backb[...]) - step0 * (cplq[...] + 2.0 * backq[...])
    arrive(*pair(fs.at[1], fr.at[1], 1))
    fr[1] = fr[1] - hs[0]
    outside = (hs[0, 0] - step0 * hs[1, 0]) * (fr[0, 0] - step0 * fr[1, 0])
    outside += (hs[0, 1] - step0 * hs[1, 1]) * (fr[0, 1] - step0 * fr[1, 1])
    send_products(1, r1b[...], cplb[...], outside)
    z = inner + outer(1)
    split_to(xs, z)
    spread(xs)
    cplq[...] = cplq[...] + backq[...] - joined(z, lam, lamx)

    def put_back(x):
        tiles = reorder([x[:, t * 128 : (t + 1) * 128] for t in range(3)], place)
        return jnp.concatenate(tiles, axis=1)

    def put_out(ref, y):
        for first, end, row in PLACES:
            ref[first:end] = y[row : row + end - first]

    inp[0:ROWS] = inp[0:ROWS] * wide(scale[0])
    fieldb[...] = put_back(r1b[...])
    norm1, product1 = products(1)
    ratio = norm1 / norm0
    step1 = norm1 / (product1 - ratio * norm1 / step0)
    put_out(x_ref, (step0 + step1 * ratio) * inp[0:ROWS] + step1 * fieldb[...])
    gamb[...] = fieldb[...] - (step1 * (1.0 + ratio) / step0) * (inp[0:ROWS] - fieldb[...])
    second = cplq[...] - flux_in(1)
    put_out(r_ref, gamb[...] + (step1 * step0) * put_back(second))

    for i in range(2):
        sent(*pair(fs.at[i], fr.at[i], i))
        sent(*flux_pair(i))
    sent(*t_pair)


def shards(right_side, capacity, base_cond, var_field, block_cols, send_list):
    n = lax.axis_size("space")
    terms, nodes = right_side.shape
    blocks, slots, area = base_cond.shape
    even, odd, expand, scales, final = chaos_tables()
    vmem = pl.BlockSpec(memory_space=pltpu.VMEM)
    field = pltpu.VMEM((ROWS, nodes), F32)
    small = pltpu.VMEM((16, nodes), F32)
    message = pltpu.VMEM((2, 2, MSG, 128), F32)
    scaled = pl.pallas_call(
        functools.partial(kernel, n),
        out_shape=(
            pltpu.VMEM((terms, nodes), F32),
            pltpu.VMEM((terms, nodes), F32),
        ),
        in_specs=[pl.BlockSpec(memory_space=pltpu.HBM)] * 10,
        out_specs=(vmem, vmem),
        scratch_shapes=[
            pltpu.VMEM((terms, nodes), F32),
            pltpu.VMEM(var_field.shape, F32),
            pltpu.VMEM(capacity.shape, F32),
            pltpu.VMEM(block_cols.shape, jnp.int32),
            pltpu.SMEM(send_list.shape, jnp.int32),
            pltpu.VMEM(even.shape, BF16),
            pltpu.VMEM(odd.shape, BF16),
            pltpu.VMEM(expand.shape, BF16),
            pltpu.VMEM(scales.shape, F32),
            pltpu.VMEM((blocks * slots, area), F32),
            pltpu.VMEM((ROWS + 16, nodes), F32),
            pltpu.VMEM((blocks, ROWS + 16, 128), F32),
            pltpu.VMEM((blocks * 16, area), F32),
            pltpu.VMEM((8 * nodes + 8, 128), F32),
            pltpu.VMEM((nodes, 2 * nodes), BF16),
            pltpu.VMEM((nodes, 2 * nodes), BF16),
            pltpu.VMEM((VARS * EVEN + 432, nodes), F32),
            pltpu.VMEM((2 * ROWS + 32, nodes), BF16),
            pltpu.VMEM((2 * ROWS, 2 * nodes), BF16),
            small, pltpu.VMEM((384, nodes), F32), small, pltpu.VMEM((384, nodes), F32), small,
            field, field, field, field, field, field, field, field,
            message, message, message, message,
            pltpu.VMEM((2, 24, 128), F32),
            pltpu.VMEM((2, 24, 128), F32),
            pltpu.VMEM((2, n, 1, 128), F32),
            pltpu.SemaphoreType.DMA((9,)),
            pltpu.SemaphoreType.DMA((4,)),
            pltpu.SemaphoreType.DMA((10,)),
            pltpu.SemaphoreType.DMA((10,)),
            pltpu.SemaphoreType.DMA((2,)),
            pltpu.SemaphoreType.DMA((2,)),
        ],
        compiler_params=pltpu.CompilerParams(
            collective_id=0, has_side_effects=True, vmem_limit_bytes=60 * 1024 * 1024
        ),
        name="galerkin_cg",
    )(
        right_side, var_field, capacity, block_cols, send_list,
        jnp.asarray(even, BF16), jnp.asarray(odd, BF16), jnp.asarray(expand, BF16), jnp.asarray(scales),
        base_cond.reshape(blocks * slots, area),
    )
    final = jnp.asarray(final)[:, None]
    return scaled[0] * final, scaled[1] * final


def solution(mesh):
    return jax.shard_map(
        shards,
        mesh=mesh,
        in_specs=(
            P(None, ("grp", "space")),
            P(("grp", "space")),
            P(("grp", "space"), None, None),
            P(None, ("grp", "space")),
            P(("grp", "space"), None),
            P(("grp", "space"), None, None),
        ),
        out_specs=(P(None, ("grp", "space")), P(None, ("grp", "space"))),
        check_vma=False,
    )
```

```python
import functools
import math

import jax
import jax.numpy as jnp
import numpy as np
from jax import lax
from jax.experimental import pallas as pl
from jax.experimental.pallas import tpu as pltpu
from jax.sharding import PartitionSpec as P

VARS = 8
ORDER = 3
ITERS = 2
SPREAD = 0.14
ROWS, EVEN, ODD, DEEP = 176, 40, 48, 56
PLACES = ((0, 1, 36), (1, 9, 48), (9, 45, 0), (45, 165, 56))
HALF = ROWS // 2
MSG = ROWS + HALF
OWN, AWAY = slice(0, 384), slice(384, 768)
MESH = pl.DeviceIdType.MESH
F32 = jnp.float32
BF16 = jnp.bfloat16


def chaos_tables():
    entries = []

    def grow(prefix, left):
        if len(prefix) == VARS:
            entries.append(tuple(prefix))
            return
        for degree in range(left + 1):
            grow(prefix + [degree], left - degree)

    grow([], ORDER)
    entries.sort(key=lambda m: (sum(m), tuple(-v for v in m)))
    lookup = {}
    for first, end, row in PLACES:
        for i in range(first, end):
            lookup[entries[i]] = row + i - first
    even = np.zeros((VARS * EVEN, 2 * (ROWS - ODD)), np.float32)
    odd = np.zeros((432, 2 * ODD), np.float32)
    expand = np.zeros((384, 16), np.float32)
    scale = np.ones((ROWS,), np.float64)
    for m, i in lookup.items():
        scale[i] = math.sqrt(math.prod(math.factorial(v) for v in m))
        held = [k for k in range(VARS) if m[k] > 0]
        for k in range(VARS):
            lowered = lookup.get(m[:k] + (m[k] - 1,) + m[k + 1 :])
            raised = lookup.get(m[:k] + (m[k] + 1,) + m[k + 1 :])
            for other, weight in ((lowered, m[k]), (raised, 1.0)):
                if other is None:
                    continue
                if i < EVEN:
                    even[EVEN * k + i, [other - ODD, ROWS - ODD + other - ODD]] = weight
                elif i < DEEP:
                    odd[8 * k + i - ODD, [other, ODD + other]] = weight
                else:
                    place = 120 * held.index(k) + i - DEEP
                    odd[64 + place, [other, ODD + other]] = weight
                    expand[place, k] = 1.0
    scales = np.stack([scale, 1.0 / scale**2], 0)
    scales = np.broadcast_to(scales[:, :, None], (2, ROWS, 128)).astype(np.float32)
    final = np.array([1.0 / scale[lookup[m]] for m in entries], np.float32)
    return even, odd, expand, scales, final


def split2(x):
    hi = x.astype(BF16)
    return hi, (x - hi.astype(F32)).astype(BF16)


def split3(x):
    hi = x.astype(BF16)
    rest = x - hi.astype(F32)
    mid = rest.astype(BF16)
    return hi, mid, (rest - mid.astype(F32)).astype(BF16)


def nn(a, b):
    return lax.dot_general(a, b, (((1,), (0,)), ((), ())), preferred_element_type=F32)


def nt(a, b):
    return lax.dot_general(a, b, (((1,), (1,)), ((), ())), preferred_element_type=F32)


def swap(x):
    return pltpu.roll(x, 64, 1)


def wide(x):
    return jnp.concatenate([x, x, x], axis=1)


def kernel(
    n,
    rhs_hbm, var_hbm, cap_hbm, cols_hbm, list_hbm, even_hbm, odd_hbm, expand_hbm, scale_hbm, base_hbm,
    x_ref, r_ref,
    rhs, var, capv, colv, lists, even, odd, expand, scale, base,
    inp, blk, wc, wf, whi, wlo, ybuf, xs, ext, lam, lamx, dmode, dmodex, caps,
    fieldb, gamb, cplb, backb, imageb, cplq, backq, r1b,
    fs, fr, hs, hr, ts, tr, allb,
    in_sem, base_sem, send_sem, recv_sem, all_send, all_recv,
):
    me = lax.axis_index("space")
    prev, nxt = lax.rem(me + n - 1, n), lax.rem(me + 1, n)
    chunk = base.shape[1] // 4

    ins = [
        pltpu.make_async_copy(src, dst, in_sem.at[i])
        for i, (src, dst) in enumerate(
            (
                (list_hbm, lists), (rhs_hbm, rhs), (var_hbm, var), (cap_hbm, capv),
                (cols_hbm, colv), (scale_hbm, scale), (even_hbm, even), (odd_hbm, odd),
                (expand_hbm, expand),
            )
        )
    ]

    def base_copy(i):
        cols = pl.ds(i * chunk, chunk)
        return pltpu.make_async_copy(base_hbm.at[:, cols], base.at[:, cols], base_sem.at[i])

    for copy in ins:
        copy.start()
    for i in range(4):
        base_copy(i).start()

    barrier = pltpu.get_barrier_semaphore()

    def greet(i, c):
        pl.semaphore_signal(
            barrier, inc=1, device_id={"space": lax.rem(me + i, n)}, device_id_type=MESH
        )
        return c

    lax.fori_loop(1, n, greet, 0)

    def remote(src, dst, which, peer):
        return pltpu.make_async_remote_copy(
            src_ref=src, dst_ref=dst, send_sem=send_sem.at[which], recv_sem=recv_sem.at[which],
            device_id={"space": peer}, device_id_type=MESH,
        )

    def pair(src, dst, e):
        return remote(src.at[0], dst.at[0], 2 * e, nxt), remote(src.at[1], dst.at[1], 2 * e + 1, prev)

    def send(up, down):
        @pl.when(me < n - 1)
        def _():
            up.start()

        @pl.when(me > 0)
        def _():
            down.start()

    def arrive(up, down):
        @pl.when(me > 0)
        def _():
            up.wait_recv()

        @pl.when(me < n - 1)
        def _():
            down.wait_recv()

    def sent(up, down):
        @pl.when(me < n - 1)
        def _():
            up.wait_send()

        @pl.when(me > 0)
        def _():
            down.wait_send()

    def left_mask(rows):
        return lax.broadcasted_iota(jnp.int32, (rows, 128), 1) < 64

    def halves(left_of, right_of):
        return jnp.where(left_mask(left_of.shape[0]), left_of, right_of)

    def pack(first_dst, last_dst, first, middle, last):
        half = middle.shape[0] // 2
        rows = first_dst.shape[0] - half
        top, low = middle[:half], middle[half:]
        first_dst[0:rows] = first[:rows]
        first_dst[rows : rows + half] = halves(top, swap(low))
        last_dst[0:rows] = last[:rows]
        last_dst[rows : rows + half] = halves(swap(top), low)

    def unpack(first_src, last_src, half):
        rows = first_src.shape[0] - half
        a, b = first_src[rows : rows + half], last_src[rows : rows + half]
        middle = jnp.concatenate([halves(a, swap(b)), halves(swap(a), b)], axis=0)
        first, last = first_src[0:rows], last_src[0:rows]
        if rows < 2 * half:
            pad = jnp.zeros((2 * half - rows, 128), F32)
            first = jnp.concatenate([first, pad], axis=0)
            last = jnp.concatenate([last, pad], axis=0)
        return first, middle, last

    @pl.when(me == 0)
    def _():
        for buf in (fr.at[0, 0], fr.at[1, 0], hr.at[0, 0], hr.at[1, 0], tr.at[0]):
            buf[...] = jnp.zeros(buf.shape, F32)

    @pl.when(me == n - 1)
    def _():
        for buf in (fr.at[0, 1], fr.at[1, 1], hr.at[0, 1], hr.at[1, 1], tr.at[1]):
            buf[...] = jnp.zeros(buf.shape, F32)

    nodes = rhs.shape[1]
    terms = rhs.shape[0]
    inp[...] = jnp.zeros_like(inp)
    for copy in ins[:4]:
        copy.wait()
    perm = [lists[0, 0, 0], lists[0, 0, 1], lists[0, 0, 2], lists[0, 1, 2], lists[0, 1, 0], lists[0, 1, 1]]
    place = []
    for r in range(6):
        at = jnp.int32(0)
        for t in range(1, 6):
            at = jnp.where(perm[t] == r, jnp.int32(t), at)
        place.append(at)
    for first, end, row in PLACES:
        inp[row : row + end - first] = rhs[first:end]
    inp[ROWS : ROWS + 8] = var[...]
    inp[ROWS + 8 : ROWS + 9] = capv[...].reshape(1, nodes)

    def reorder(tiles, index):
        rows = tiles[0].shape[0]
        for t in range(3):
            other = swap(tiles[t])
            blk[2 * t, 0:rows] = halves(tiles[t], other)
            blk[2 * t + 1, 0:rows] = halves(other, tiles[t])
        return [halves(blk[index[2 * t], 0:rows], blk[index[2 * t + 1], 0:rows]) for t in range(3)]

    moved = reorder([inp[:, t * 128 : (t + 1) * 128] for t in range(3)], perm)
    ins[5].wait()
    for t in range(3):
        cols = slice(t * 128, (t + 1) * 128)
        fieldb[:, cols] = moved[t][:ROWS] * scale[0]
        lam[0:8, cols] = moved[t][ROWS : ROWS + 8] * SPREAD
        caps[0:8, cols] = moved[t][ROWS + 8 : ROWS + 16]
    lam[8:9] = jnp.ones((1, nodes), F32)
    lam[9:16] = jnp.zeros((7, nodes), F32)
    cap = caps[0:1]

    pl.semaphore_wait(barrier, n - 1)

    def send_field(i, x):
        pack(fs.at[i, 0], fs.at[i, 1], x[:, 0:128], x[:, 128:256], x[:, 256:384])
        send(*pair(fs.at[i], fr.at[i], i))

    send_field(0, fieldb[...])

    def split_to(dst, x, cols=slice(None)):
        h, l = split2(x)
        dst[0:ROWS, cols] = h
        dst[ROWS : 2 * ROWS, cols] = l

    def spread(src):
        cols = OWN
        up = jnp.concatenate([src[ODD:ROWS, cols], src[ROWS + ODD : 2 * ROWS, cols]], axis=0)
        down = jnp.concatenate([src[0:ODD, cols], src[ROWS : ROWS + ODD, cols]], axis=0)
        ybuf[0 : VARS * EVEN] = nn(even[...], up)
        ybuf[VARS * EVEN :] = nn(odd[...], down)

    def joined(x, w, wx):
        top = w[8:9] * x[0:EVEN]
        one = w[8:9] * x[ODD:DEEP]
        low = w[8:9] * x[DEEP:ROWS]
        ones_at = VARS * EVEN
        for k in range(VARS):
            top = top + w[k : k + 1] * ybuf[EVEN * k : EVEN * (k + 1)]
            one = one + w[k : k + 1] * ybuf[ones_at + 8 * k : ones_at + 8 * (k + 1)]
        deep_at = ones_at + 64
        for s in range(3):
            low = low + wx[120 * s : 120 * s + 120] * ybuf[deep_at + 120 * s : deep_at + 120 * s + 120]
        return jnp.concatenate([top, jnp.zeros((ODD - EVEN, nodes), F32), one, low], axis=0)

    def expanded(w):
        h, m, l = split3(w[...])
        e = expand[...]
        return nn(e, h) + (nn(e, m) + nn(e, l))

    ins[6].wait()
    ins[7].wait()
    ins[8].wait()
    lamx[...] = expanded(lam)
    split_to(ext, fieldb[...], OWN)
    spread(ext)
    gamb[...] = joined(fieldb[...], lam, lamx)

    rowsc, rowse = wc.shape[0], base.shape[0]
    ins[4].wait()
    slots = rowse // 6
    lane = lax.broadcasted_iota(jnp.int32, (1, rowse), 1)
    owner = jnp.zeros((1, rowse), jnp.int32)
    for j in range(1, 6):
        owner = owner + jnp.where(lane >= slots * j, 1, 0)
    slot = lane - slots * owner
    repeat = lax.broadcasted_iota(jnp.int32, (slots - 1, rowse), 0) == slot - 1
    given = nn(colv[...].astype(F32).astype(BF16), repeat.astype(F32).astype(BF16))
    given = jnp.where(lax.broadcasted_iota(jnp.int32, given.shape, 0) == owner, given, 0.0)
    column = jnp.sum(given, axis=0, keepdims=True).astype(jnp.int32)
    column = jnp.where(slot == 0, owner, column)
    where = jnp.where(column < 9, column, jnp.where(column == 11, 9, column + 1))
    row = jnp.zeros((1, rowse), jnp.int32)
    for j in range(6):
        where = jnp.where(column == j, place[j], where)
        row = jnp.where(owner == j, place[j], row)
    target = row * 16 + (where & 1) * 8 + (where >> 1)
    pick = (
        lax.broadcasted_iota(jnp.int32, (rowsc, rowse), 0) == target
    ).astype(F32).astype(BF16)
    for i in range(4):
        base_copy(i).wait()
        for j in range(2):
            cols = slice(i * chunk + j * 512, i * chunk + j * 512 + 512)
            h, l = split2(base[:, cols])
            wc[:, cols] = nn(pick, h) + nn(pick, l)

    def lay(j, c):
        cols = slice(j * 128, j * 128 + 128)
        for t in range(6):
            even = wc[t * 16 : t * 16 + 8, cols]
            odd = wc[t * 16 + 8 : t * 16 + 16, cols]
            wf[pl.ds(t * 64 + 2 * j, 8, stride=nodes + 1), :] = halves(even, swap(odd))
            wf[pl.ds(t * 64 + 2 * j + 1, 8, stride=nodes + 1), :] = halves(swap(even), odd)
        return c

    for j in range(32):
        lay(j, 0)
    for q in (3, 4, 5, 0, 1, 2):
        h, l = split2(wf[q * (nodes + 1) : q * (nodes + 1) + nodes])
        whi[:, q * 128 : (q + 1) * 128] = h
        wlo[:, q * 128 : (q + 1) * 128] = l

    t_pair = (remote(ts.at[1], tr.at[0], 8, nxt), remote(ts.at[0], tr.at[1], 9, prev))

    def edges(src, cols, dot):
        left = src[0 : 2 * ROWS, cols] if dot is nt else src[0 : 2 * ROWS]
        both = dot(left, whi[:, cols])
        return both[0:ROWS] + both[ROWS : 2 * ROWS] + dot(left[0:ROWS], wlo[:, cols])

    def flux_pair(i):
        to_prev = remote(hs.at[i, 0], hr.at[i, 1], 2 * (2 + i) + 1, prev)
        to_next = remote(hs.at[i, 1], hr.at[i, 0], 2 * (2 + i), nxt)
        return to_next, to_prev

    def flux_and_weights(cols):
        fine = nn(xs[...], whi[:, cols])
        rest = jnp.concatenate([xs[0:ROWS], xs[2 * ROWS : 2 * ROWS + 16]], axis=0)
        rest = nn(rest, wlo[:, cols])
        return (
            fine[0:ROWS] + fine[ROWS : 2 * ROWS] + rest[0:ROWS],
            fine[2 * ROWS : 2 * ROWS + 16] + fine[2 * ROWS + 16 :] + rest[ROWS:],
        )

    def send_flux(i, flux):
        pack(hs.at[i, 0], hs.at[i, 1], flux[:, 0:128], flux[:, 128:256], flux[:, 256:384])
        send(*flux_pair(i))

    def outer(i):
        for t, tile in enumerate(unpack(fr.at[i, 0], fr.at[i, 1], HALF)):
            split_to(ext, tile, slice(384 + t * 128, 512 + t * 128))
        return edges(ext, AWAY, nt)

    def flux_in(i):
        arrive(*flux_pair(i))
        return jnp.concatenate(unpack(hr.at[i, 1], hr.at[i, 0], HALF), axis=1)

    def fold(x):
        total = x[0:8]
        for i in range(1, x.shape[0] // 8):
            total = total + x[8 * i : 8 * i + 8]
        return total

    def fold_wide(x):
        return fold(x[:, 0:128] + x[:, 128:256] + x[:, 256:384])

    def all_copy(i, off):
        return pltpu.make_async_remote_copy(
            src_ref=allb.at[i, me], dst_ref=allb.at[i, me],
            send_sem=all_send.at[i], recv_sem=all_recv.at[i],
            device_id={"space": lax.rem(me + off, n)}, device_id_type=MESH,
        )

    def send_products(i, x, rest, outside):
        weight = scale[1]
        packed = jnp.concatenate([weight, halves(weight[:HALF], weight[HALF:])], axis=0)
        weight = wide(weight)
        norm = jnp.sum(fold_wide(x * x * weight), axis=0, keepdims=True)
        product = fold_wide(x * rest * weight) - 2.0 * fold(outside * packed)
        product = jnp.sum(product, axis=0, keepdims=True)
        allb[i, me] = halves(norm + swap(norm), product + swap(product))

        def go(off, c):
            all_copy(i, off).start()
            return c

        lax.fori_loop(1, n, go, 0)

    def products(i):
        others = allb.at[i, pl.ds(0, n - 1)]
        pltpu.make_async_copy(others, others, all_recv.at[i]).wait()
        pltpu.make_async_copy(others, others, all_send.at[i]).wait()
        total = allb[i, 0]
        for d in range(1, n):
            total = total + allb[i, d]
        left = left_mask(1)
        return (
            jnp.sum(jnp.where(left, total, 0.0), keepdims=True),
            jnp.sum(jnp.where(left, 0.0, total), keepdims=True),
        )

    split_to(xs, gamb[...])
    h, l = split2(lam[...])
    xs[2 * ROWS : 2 * ROWS + 16] = h
    xs[2 * ROWS + 16 : 2 * ROWS + 32] = l
    flux, toward = flux_and_weights(AWAY)
    pack(ts.at[0], ts.at[1], toward[:, 0:128], toward[:, 128:256], toward[:, 256:384])
    send(*t_pair)
    send_flux(0, flux)
    flux, toward = flux_and_weights(OWN)
    backb[...] = -flux
    inner = edges(ext, OWN, nt)
    ones = jnp.ones((16, 768), BF16)
    row_total = (nt(ones, whi[...]) + nt(ones, wlo[...]))[0:1]
    arrive(*t_pair)
    came = jnp.concatenate(unpack(tr.at[1], tr.at[0], 8), axis=1)
    dmode[...] = toward + came + row_total * lam[...] + jnp.where(
        lax.broadcasted_iota(jnp.int32, (16, nodes), 0) == 8, cap, 0.0
    )
    dmodex[...] = expanded(dmode)
    cplb[...] = joined(fieldb[...], dmode, dmodex)
    arrive(*pair(fs.at[0], fr.at[0], 0))
    z = inner + outer(0)
    split_to(xs, z)
    spread(xs)
    imageb[...] = cplb[...] + backb[...] - joined(z, lam, lamx)
    send_field(1, imageb[...])
    send_products(
        0, fieldb[...], cplb[...] + 2.0 * backb[...], hs[0, 0] * fr[0, 0] + hs[0, 1] * fr[0, 1]
    )
    imageb[...] -= flux_in(0)

    split_to(ext, imageb[...], OWN)
    spread(ext)
    split_to(xs, joined(imageb[...], lam, lamx))
    send_flux(1, edges(xs, AWAY, nn))
    cplq[...] = joined(imageb[...], dmode, dmodex)
    backq[...] = -edges(xs, OWN, nn)
    inner = edges(ext, OWN, nt)
    norm0, product0 = products(0)
    step0 = norm0 / product0
    r1b[...] = fieldb[...] - step0 * imageb[...]
    cplb[...] = (cplb[...] + 2.0 * backb[...]) - step0 * (cplq[...] + 2.0 * backq[...])
    arrive(*pair(fs.at[1], fr.at[1], 1))
    fr[1] = fr[1] - hs[0]
    outside = (hs[0, 0] - step0 * hs[1, 0]) * (fr[0, 0] - step0 * fr[1, 0])
    outside += (hs[0, 1] - step0 * hs[1, 1]) * (fr[0, 1] - step0 * fr[1, 1])
    send_products(1, r1b[...], cplb[...], outside)
    z = inner + outer(1)
    split_to(xs, z)
    spread(xs)
    cplq[...] = cplq[...] + backq[...] - joined(z, lam, lamx)

    def put_back(x):
        tiles = reorder([x[:, t * 128 : (t + 1) * 128] for t in range(3)], place)
        return jnp.concatenate(tiles, axis=1)

    def put_out(ref, y):
        for first, end, row in PLACES:
            ref[first:end] = y[row : row + end - first]

    inp[0:ROWS] = inp[0:ROWS] * wide(scale[0])
    fieldb[...] = put_back(r1b[...])
    norm1, product1 = products(1)
    ratio = norm1 / norm0
    step1 = norm1 / (product1 - ratio * norm1 / step0)
    put_out(x_ref, (step0 + step1 * ratio) * inp[0:ROWS] + step1 * fieldb[...])
    gamb[...] = fieldb[...] - (step1 * (1.0 + ratio) / step0) * (inp[0:ROWS] - fieldb[...])
    second = cplq[...] - flux_in(1)
    put_out(r_ref, gamb[...] + (step1 * step0) * put_back(second))

    for i in range(2):
        sent(*pair(fs.at[i], fr.at[i], i))
        sent(*flux_pair(i))
    sent(*t_pair)


def shards(right_side, capacity, base_cond, var_field, block_cols, send_list):
    n = lax.axis_size("space")
    terms, nodes = right_side.shape
    blocks, slots, area = base_cond.shape
    even, odd, expand, scales, final = chaos_tables()
    vmem = pl.BlockSpec(memory_space=pltpu.VMEM)
    field = pltpu.VMEM((ROWS, nodes), F32)
    small = pltpu.VMEM((16, nodes), F32)
    message = pltpu.VMEM((2, 2, MSG, 128), F32)
    scaled = pl.pallas_call(
        functools.partial(kernel, n),
        out_shape=(
            pltpu.VMEM((terms, nodes), F32),
            pltpu.VMEM((terms, nodes), F32),
        ),
        in_specs=[pl.BlockSpec(memory_space=pltpu.HBM)] * 10,
        out_specs=(vmem, vmem),
        scratch_shapes=[
            pltpu.VMEM((terms, nodes), F32),
            pltpu.VMEM(var_field.shape, F32),
            pltpu.VMEM(capacity.shape, F32),
            pltpu.VMEM(block_cols.shape, jnp.int32),
            pltpu.SMEM(send_list.shape, jnp.int32),
            pltpu.VMEM(even.shape, BF16),
            pltpu.VMEM(odd.shape, BF16),
            pltpu.VMEM(expand.shape, BF16),
            pltpu.VMEM(scales.shape, F32),
            pltpu.VMEM((blocks * slots, area), F32),
            pltpu.VMEM((ROWS + 16, nodes), F32),
            pltpu.VMEM((blocks, ROWS + 16, 128), F32),
            pltpu.VMEM((blocks * 16, area), F32),
            pltpu.VMEM((8 * nodes + 8, 128), F32),
            pltpu.VMEM((nodes, 2 * nodes), BF16),
            pltpu.VMEM((nodes, 2 * nodes), BF16),
            pltpu.VMEM((VARS * EVEN + 432, nodes), F32),
            pltpu.VMEM((2 * ROWS + 32, nodes), BF16),
            pltpu.VMEM((2 * ROWS, 2 * nodes), BF16),
            small, pltpu.VMEM((384, nodes), F32), small, pltpu.VMEM((384, nodes), F32), small,
            field, field, field, field, field, field, field, field,
            message, message, message, message,
            pltpu.VMEM((2, 24, 128), F32),
            pltpu.VMEM((2, 24, 128), F32),
            pltpu.VMEM((2, n, 1, 128), F32),
            pltpu.SemaphoreType.DMA((9,)),
            pltpu.SemaphoreType.DMA((4,)),
            pltpu.SemaphoreType.DMA((10,)),
            pltpu.SemaphoreType.DMA((10,)),
            pltpu.SemaphoreType.DMA((2,)),
            pltpu.SemaphoreType.DMA((2,)),
        ],
        compiler_params=pltpu.CompilerParams(
            collective_id=0, has_side_effects=True, vmem_limit_bytes=60 * 1024 * 1024
        ),
        name="galerkin_cg",
    )(
        right_side, var_field, capacity, block_cols, send_list,
        jnp.asarray(even, BF16), jnp.asarray(odd, BF16), jnp.asarray(expand, BF16), jnp.asarray(scales),
        base_cond.reshape(blocks * slots, area),
    )
    final = jnp.asarray(final)[:, None]
    return scaled[0] * final, scaled[1] * final


def solution(mesh):
    return jax.shard_map(
        shards,
        mesh=mesh,
        in_specs=(
            P(None, ("grp", "space")),
            P(("grp", "space")),
            P(("grp", "space"), None, None),
            P(None, ("grp", "space")),
            P(("grp", "space"), None),
            P(("grp", "space"), None, None),
        ),
        out_specs=(P(None, ("grp", "space")), P(None, ("grp", "space"))),
        check_vma=False,
    )
```
